32 devices in a mesh: dp: 32 (over z, y, x, core), mp: 1.
Axes of the slice: x: 2, y: 2, z: 4, core: 2. Of those that a mesh axis runs over, the one named last changes fastest.
Arguments:
- features: bfloat16 [131072, 1024], P('dp'), may hold values from -6 to 6
- w_in: bfloat16 [1024, 1024], P(None, 'mp'), may hold values from -0.1875 to 0.1875
- w_out: bfloat16 [1024, 128], P('mp'), may hold values from -0.1875 to 0.1875
- send_rows: int32 [65536], P(('dp', 'mp')), may hold values from 0 to 4095
- pair_src: int32 [131072, 16], P(('dp', 'mp')), may hold values from 0 to 2047
- pair_weight: float32 [131072, 16], P(('dp', 'mp')), may hold values from 0.1 to 1
- pair_mask: int32 [131072, 16], P(('dp', 'mp')), may hold values 0 or 1
Outputs:
- grad_in: float32 [1024, 1024], P(None, 'mp')
- grad_out: float32 [1024, 128], P('mp')
The draws below stay inside these ranges and needn't reach their ends.
Inputs may be any that keep to these rules, and one draw needn't show every extreme that they name: `send_rows`: local row indices of the sending device.
All inputs are finite; a program needn't handle non-finite values. No bound on the sum of `pair_mask` on one device may be relied on, other than what follows from the above.
Results may differ from the reference program's by a relative error of at most 0.0062.
Values may be sent and summed in bfloat16 or wider, within the bound.
No kernel may reach another device: no remote copies, remote signals or barrier semaphores. Data moves between devices by JAX's collectives and lax.ppermute only.
A program may use at most 192 MiB of HBM per device.

```python
import math
import jax
import jax.numpy as jnp
from jax import lax

DIN = 1024
H = 1024
K = 128
P_SIZE = 16
NODE_DEV = 4096
RECV_DEV = 2048
NODES = 131072
ROWS = 4096
SLOTS = 64
SENDS = 65536
N_DP = 32
N_MP = 1


def touch_ends(values, own_key, smallest, largest):
    longest = values.shape.index(max(values.shape))
    spots = []
    for shift in (0, 1):
        where = [jax.random.randint(jax.random.fold_in(own_key, axis), (), 0, length) for axis, length in enumerate(values.shape)]
        where[longest] = (where[longest] + shift) % values.shape[longest]
        spots.append(tuple(where))
    return values.at[spots[0]].set(smallest).at[spots[1]].set(largest)


def block_scale(key, shape, cuts, smallest, largest):
    factor_of, own = 1.0, jax.random.fold_in(key, 6)
    for position, parts in cuts:
        steps = jnp.exp(jax.random.uniform(jax.random.fold_in(own, position), (parts,), jnp.float32, smallest / len(cuts), largest / len(cuts)))
        factor_of = factor_of * jnp.repeat(steps, shape[position] // parts).reshape([-1 if axis == position else 1 for axis in range(len(shape))])
    return factor_of


def noise(rng, extent, deviation, bound, split=(), held_as=jnp.bfloat16):
    result = jax.random.normal(rng, extent, jnp.float32) * deviation
    if len(split) > 0:
        result = block_scale(rng, extent, split, -0.22, 0.18) * result
    return jnp.clip(result, min=-bound, max=bound).astype(held_as)


def setup_inputs(seed: int = 0) -> dict:
    splits = jax.random.split(jax.random.key(seed), 8)
    return {
        "features": noise(splits[0], (NODES, DIN), 1.0, 6.0, ((0, 32),)),
        "w_in": noise(splits[1], (DIN, H), DIN ** -0.5, 0.1875),
        "w_out": noise(splits[2], (H, K), H ** -0.5, 0.1875),
        "send_rows": touch_ends(jax.random.randint(splits[3], (SENDS,), 0, ROWS), jax.random.fold_in(splits[3], 1), 0, ROWS - 1).astype(jnp.int32),
        "pair_src": touch_ends(jax.random.randint(splits[4], (NODES, P_SIZE), 0, RECV_DEV), jax.random.fold_in(splits[4], 1), 0, RECV_DEV - 1).astype(jnp.int32),
        "pair_weight": jnp.clip(jnp.exp(math.log(1.0) - 2.3025851 * jax.random.uniform(splits[5], (NODES, P_SIZE), jnp.float32) ** block_scale(splits[5], (NODES, P_SIZE), ((0, 32),), -0.2, 0.2)), 0.1, 1.0),
        "pair_mask": touch_ends((jax.random.randint(splits[6], (NODES, P_SIZE), 0, 4) < 3).astype(jnp.int32), jax.random.fold_in(splits[6], 1), 0, 1),
    }


def reference(features, w_in, w_out, send_rows, pair_src, pair_weight, pair_mask):
    high = lax.Precision.HIGHEST
    blocks = features.reshape(N_DP, NODE_DEV, DIN)

    def forward(block):
        hidden = jax.nn.silu(jnp.dot(block.astype(jnp.float32), w_in.astype(jnp.float32), preferred_element_type=jnp.float32)).astype(jnp.bfloat16)
        return jnp.dot(hidden.astype(jnp.float32), w_out.astype(jnp.float32), preferred_element_type=jnp.float32)
    embed = lax.map(forward, blocks).reshape(NODES, K)
    gram = jnp.dot(embed.T, embed, precision=high) / NODES
    chol = jnp.linalg.cholesky(gram)
    white = lax.linalg.triangular_solve(chol, embed, left_side=False, lower=True, transpose_a=True)
    shards = N_DP * N_MP
    dev = jnp.arange(shards, dtype=jnp.int32)[:, None]
    slot = jnp.arange(RECV_DEV, dtype=jnp.int32)[None, :]
    source = slot // SLOTS * N_MP + dev % N_MP
    local_idx = send_rows[source * RECV_DEV + dev // N_MP * SLOTS + slot % SLOTS]
    table = (source * ROWS + local_idx).astype(jnp.int32)
    scale = 1.0 / (P_SIZE * math.sqrt(NODES))
    coef = pair_weight * pair_mask.astype(jnp.float32) * scale

    def visit(acc, item):
        rows_z, src, cs, tab = item
        partner = tab[src]
        diff = rows_z[:, None, :] - white[partner]
        own = 2.0 * lax.optimization_barrier(jnp.sum(cs[:, :, None] * diff, axis=1))
        acc = acc.at[partner.reshape(-1)].add((-2.0 * cs[:, :, None] * diff).reshape(-1, K))
        return (acc, own)
    init = jnp.zeros((NODES, K), jnp.float32)
    acc, owns = lax.scan(visit, init, (white.reshape(shards, ROWS, K), pair_src.reshape(shards, ROWS, P_SIZE), coef.reshape(shards, ROWS, P_SIZE), table))
    grad_z = owns.reshape(NODES, K) + acc
    curv = jnp.dot(white.T, grad_z, precision=high)
    inner = grad_z - jnp.dot(white, curv, precision=high) / NODES
    grad_y = lax.linalg.triangular_solve(chol, inner, left_side=False, lower=True, transpose_a=False).astype(jnp.bfloat16)

    def backward(carry, item):
        block, gy = item
        pre = jnp.dot(block.astype(jnp.float32), w_in.astype(jnp.float32), preferred_element_type=jnp.float32)
        hidden = jax.nn.silu(pre).astype(jnp.bfloat16)
        g_out = carry[1] + jnp.dot(hidden.T.astype(jnp.float32), gy.astype(jnp.float32), preferred_element_type=jnp.float32)
        dh = jnp.dot(gy.astype(jnp.float32), w_out.T.astype(jnp.float32), preferred_element_type=jnp.float32)
        sig = jax.nn.sigmoid(pre)
        grad_pre = (dh * sig * (1.0 + pre * (1.0 - sig))).astype(jnp.bfloat16)
        g_in = carry[0] + jnp.dot(block.T.astype(jnp.float32), grad_pre.astype(jnp.float32), preferred_element_type=jnp.float32)
        return ((g_in, g_out), None)
    start = (jnp.zeros((DIN, H), jnp.float32), jnp.zeros((H, K), jnp.float32))
    (grad_in, grad_out), _ = lax.scan(backward, start, (blocks, grad_y.reshape(N_DP, NODE_DEV, K)))
    return (grad_in, grad_out)
```

```python
import functools
import math

import jax
import jax.numpy as jnp
from jax import lax
from jax.experimental import pallas as pl
from jax.experimental.pallas import tpu as pltpu
from jax.sharding import PartitionSpec as P

F32 = jnp.float32
BF16 = jnp.bfloat16
LANES = 128
WIDE = 256
STEPS = 8
VMEM_BYTES = 56 * 1024 * 1024


def params(steps=1):
    return pltpu.CompilerParams(
        dimension_semantics=("arbitrary",) * steps, vmem_limit_bytes=VMEM_BYTES
    )


def cost(flops, read):
    return pl.CostEstimate(flops=int(flops), bytes_accessed=int(read), transcendentals=0)


def dot_tn(a, b):
    return lax.dot_general(a, b, (((0,), (0,)), ((), ())), preferred_element_type=F32)


def dot_nt(a, b):
    return lax.dot_general(a, b, (((1,), (1,)), ((), ())), preferred_element_type=F32)


def dot(a, b):
    return jnp.dot(a, b, preferred_element_type=F32)


def forward_kernel(x_ref, w_in_ref, w_out_ref, hidden_ref, slope_ref, y_ref):
    units = w_in_ref.shape[1]
    step = min(512, units)
    x = x_ref[...]
    for at in range(0, units, step):
        pre = dot(x, w_in_ref[:, at:at + step])
        sig = jax.nn.sigmoid(pre)
        act = pre * sig
        hidden_ref[:, at:at + step] = act.astype(BF16)
        slope_ref[:, at:at + step] = sig + act * (1.0 - sig)
    y_ref[...] = dot(hidden_ref[...], w_out_ref[...]).astype(y_ref.dtype)


def forward(features, w_in, w_out, y_type):
    nodes, din = features.shape
    units = w_in.shape[1]
    width = w_out.shape[1]
    tile = min(1024, nodes)
    return pl.pallas_call(
        forward_kernel,
        grid=(nodes // tile,),
        in_specs=[
            pl.BlockSpec((tile, din), lambda i: (i, 0)),
            pl.BlockSpec((din, units), lambda i: (0, 0)),
            pl.BlockSpec((units, width), lambda i: (0, 0)),
        ],
        out_specs=[
            pl.BlockSpec((tile, units), lambda i: (i, 0)),
            pl.BlockSpec((tile, units), lambda i: (i, 0)),
            pl.BlockSpec((tile, width), lambda i: (i, 0)),
        ],
        out_shape=[
            jax.ShapeDtypeStruct((nodes, units), BF16),
            jax.ShapeDtypeStruct((nodes, units), F32),
            jax.ShapeDtypeStruct((nodes, width), y_type),
        ],
        compiler_params=params(),
        cost_estimate=cost(2 * nodes * units * (din + width), 2 * nodes * (din + 2 * units)),
        name="forward",
    )(features, w_in, w_out)


def send_kernel(y_ref, index_ref, sent_ref, gram_ref):
    rows = y_ref.shape[0]
    y = y_ref[...]
    gram_ref[...] = dot_tn(y, y)
    columns = index_ref[...].T
    each = 4 if index_ref.shape[0] % 4 == 0 else 1
    place = lax.broadcasted_iota(jnp.int32, (LANES, rows), 1)
    for at in range(0, index_ref.shape[0], each):
        spots = [
            jnp.where(place == columns[:, k:k + 1], 1.0, 0.0).astype(BF16)
            for k in range(at, at + each)
        ]
        spots = jnp.concatenate(spots, axis=0)
        sent_ref[at * LANES:(at + each) * LANES, :] = dot(spots, y).astype(BF16)


def send(y, send_rows):
    rows, width = y.shape
    count = send_rows.shape[0]
    return pl.pallas_call(
        send_kernel,
        out_shape=[
            jax.ShapeDtypeStruct((count, width), BF16),
            jax.ShapeDtypeStruct((width, width), F32),
        ],
        compiler_params=pltpu.CompilerParams(vmem_limit_bytes=VMEM_BYTES),
        cost_estimate=cost(2 * rows * count * width, 2 * width * (rows + count)),
        name="send",
    )(y, send_rows.reshape(count // LANES, LANES))


def weights_kernel(pairs, first, *refs):
    if first:
        src_ref, coef_ref, y_ref, weights_ref, scaled_ref, back_ref, square_ref = refs
    else:
        src_ref, coef_ref, y_ref, back_in, square_in = refs[:5]
        weights_ref, scaled_ref, back_ref, square_ref = refs[5:]
    groups, per = src_ref.shape
    count = weights_ref.shape[1]
    members = per // pairs
    high = count // WIDE

    @pl.when(pl.program_id(0) == 0)
    def _():
        if first:
            back_ref[...] = jnp.zeros_like(back_ref)
            square_ref[...] = jnp.zeros_like(square_ref)
        else:
            back_ref[...] = back_in[...]
            square_ref[...] = square_in[...]

    member = lax.broadcasted_iota(jnp.int32, (1, per), 1) // pairs
    row = lax.broadcasted_iota(jnp.int32, (high * members, per), 0)
    lane = lax.broadcasted_iota(jnp.int32, (WIDE, per), 0)
    for g in range(groups):
        src = src_ref[g:g + 1, :]
        target = (src // WIDE) * members + member
        left = jnp.where(row == target, coef_ref[g:g + 1, :], 0.0).astype(BF16)
        right = jnp.where(lane == src % WIDE, 1.0, 0.0).astype(BF16)
        part = dot_nt(left, right).astype(BF16)
        sums = None
        at = slice(g * members, (g + 1) * members)
        for h in range(high):
            piece = part[h * members:(h + 1) * members, :]
            weights_ref[at, h * WIDE:(h + 1) * WIDE] = piece
            sums = piece.astype(F32) if sums is None else sums + piece.astype(F32)
        scaled_ref[at, :] = jnp.sum(sums, axis=1, keepdims=True) * y_ref[at, :].astype(F32)
    y = y_ref[...]
    left = jnp.concatenate([y.astype(F32).T.astype(BF16), jnp.ones((16, y.shape[0]), BF16)], axis=0)
    back_ref[...] += dot(left, weights_ref[...])
    square_ref[...] += dot_tn(y, scaled_ref[...].astype(BF16))


def weights_of(src, coef, y, carry, pairs, count, part, parts):
    rows, width = y.shape[0] // parts, y.shape[1]
    per = src.shape[1]
    members = per // pairs
    groups = min(16, src.shape[0] // parts)
    tile = groups * members
    skip = part * (rows // tile)
    sums = [
        jax.ShapeDtypeStruct((width + 16, count), F32),
        jax.ShapeDtypeStruct((width, width), F32),
    ]
    sum_specs = [pl.BlockSpec(x.shape, lambda i: (0, 0)) for x in sums]
    return pl.pallas_call(
        functools.partial(weights_kernel, pairs, part == 0),
        grid=(rows // tile,),
        in_specs=[
            pl.BlockSpec((groups, per), lambda i: (i + skip, 0)),
            pl.BlockSpec((groups, per), lambda i: (i + skip, 0)),
            pl.BlockSpec((tile, width), lambda i: (i + skip, 0)),
        ]
        + (sum_specs if part else []),
        out_specs=[
            pl.BlockSpec((tile, count), lambda i: (i, 0)),
            pl.BlockSpec((tile, width), lambda i: (i, 0)),
        ]
        + sum_specs,
        out_shape=[
            jax.ShapeDtypeStruct((rows, count), BF16),
            jax.ShapeDtypeStruct((rows, width), F32),
        ]
        + sums,
        compiler_params=params(),
        cost_estimate=cost(4 * rows * count * width, 2 * rows * count),
        name="weights",
    )(src, coef, y, *carry)


def back_kernel(got_ref, sums_ref, square_ref, back_ref, spread_ref):
    width = got_ref.shape[1]
    got = got_ref[...]
    sums = sums_ref[...].T
    back = (sums[:, width:width + 1] * got.astype(F32) - sums[:, :width]).astype(BF16)
    back_ref[...] = back
    cross = dot(sums_ref[:width, :].astype(BF16), got)
    spread_ref[...] = square_ref[...] - cross + dot_tn(got, back)


def back_of(got, sums, square):
    count, width = got.shape
    return pl.pallas_call(
        back_kernel,
        out_shape=[
            jax.ShapeDtypeStruct((count, width), BF16),
            jax.ShapeDtypeStruct((width, width), F32),
        ],
        compiler_params=pltpu.CompilerParams(vmem_limit_bytes=VMEM_BYTES),
        cost_estimate=cost(4 * count * width * width, 6 * count * width),
        name="back",
    )(got, sums, square)


def own_kernel(parts, nodes, *refs):
    weights_refs = refs[:parts]
    scaled_refs = refs[parts:2 * parts]
    got_ref, gram_ref, own_ref, inverse_ref = refs[2 * parts:]
    steps = pl.num_programs(0)
    each = steps // parts
    width = gram_ref.shape[0]
    split_by = width // STEPS

    @pl.when(pl.program_id(0) == 0)
    def _():
        inverse_ref[...] = gram_ref[...] * (1.0 / nodes)

    for part in range(parts):

        @pl.when(pl.program_id(0) // each == part)
        def _():
            own_ref[...] = scaled_refs[part][...] - dot(weights_refs[part][...], got_ref[...])
            matrix = inverse_ref[...]
            matrix = eliminate(matrix, pl.program_id(0) * split_by, split_by)
            inverse_ref[...] = matrix


def eliminate(matrix, start, count):
    width = matrix.shape[0]
    rows = lax.broadcasted_iota(jnp.int32, (width, width), 0)
    lanes = lax.broadcasted_iota(jnp.int32, (width, width), 1)
    for step in range(count):
        k = start + step
        at_row = rows == k
        at_lane = lanes == k
        row = jnp.sum(jnp.where(at_row, matrix, 0.0), axis=0, keepdims=True)
        column = jnp.sum(jnp.where(at_lane, matrix, 0.0), axis=1, keepdims=True)
        pivot = 1.0 / jnp.sum(jnp.where(at_lane[:1], row, 0.0), axis=1, keepdims=True)
        scaled = jnp.where(at_lane[:1], pivot, row * pivot)
        rest = jnp.where(at_lane, 0.0, matrix) - column * scaled
        matrix = jnp.where(at_row, scaled, rest)
    return matrix


def part_block(tile, count, part, each):
    return pl.BlockSpec((tile, count), lambda i: (jnp.clip(i - part * each, 0, each - 1), 0))


def own_of(weights, scaled, got, gram, nodes):
    count, width = got.shape
    parts = len(weights)
    rows = weights[0].shape[0] * parts
    tile = rows // STEPS
    each = STEPS // parts
    return pl.pallas_call(
        functools.partial(own_kernel, parts, nodes),
        grid=(STEPS,),
        in_specs=[part_block(tile, count, part, each) for part in range(parts)]
        + [part_block(tile, width, part, each) for part in range(parts)]
        + [
            pl.BlockSpec((count, width), lambda i: (0, 0)),
            pl.BlockSpec((width, width), lambda i: (0, 0)),
        ],
        out_specs=[
            pl.BlockSpec((tile, width), lambda i: (i, 0)),
            pl.BlockSpec((width, width), lambda i: (0, 0)),
        ],
        out_shape=[
            jax.ShapeDtypeStruct((rows, width), F32),
            jax.ShapeDtypeStruct((width, width), F32),
        ],
        compiler_params=params(),
        cost_estimate=cost(2 * rows * count * width, 2 * rows * count),
        name="own",
    )(*weights, *scaled, got, gram)


def split(value):
    first = value.astype(BF16)
    return first, (value - first.astype(F32)).astype(BF16)


def grad_y_kernel(
    nodes, scale, own_ref, y_ref, index_ref, returned_ref, inverse_ref, spread_ref, out_ref, right_ref
):
    tile, width = own_ref.shape
    count = returned_ref.shape[0]

    @pl.when(pl.program_id(0) == 0)
    def _():
        high = lax.Precision.HIGHEST
        inverse = inverse_ref[...]
        half = jnp.dot(inverse, spread_ref[...], precision=high, preferred_element_type=F32)
        sandwich = jnp.dot(half, inverse, precision=high, preferred_element_type=F32)
        for at, value in ((0, 2.0 * scale * inverse), (width, -2.0 * scale / nodes * sandwich)):
            first, second = split(value)
            right_ref[at:at + width, :width] = first
            right_ref[at:at + width, width:] = second

    at = lax.broadcasted_iota(jnp.int32, (tile, count), 0) + pl.program_id(0) * tile
    spots = jnp.where(at == index_ref[...], 1.0, 0.0).astype(BF16)
    nearby = own_ref[...] + dot(spots, returned_ref[...])
    first, second = split(nearby)
    both = dot(jnp.concatenate([first, y_ref[...]], axis=1), right_ref[...])
    total = both[:, :width] + both[:, width:] + dot(second, right_ref[:width, :width])
    out_ref[...] = total.astype(BF16)


def grad_y_of(own, y, send_rows, returned, inverse, spread, nodes, scale):
    rows, width = y.shape
    count = returned.shape[0]
    tile = min(512, rows)
    return pl.pallas_call(
        functools.partial(grad_y_kernel, nodes, scale),
        grid=(rows // tile,),
        in_specs=[
            pl.BlockSpec((tile, width), lambda i: (i, 0)),
            pl.BlockSpec((tile, width), lambda i: (i, 0)),
            pl.BlockSpec((1, count), lambda i: (0, 0)),
            pl.BlockSpec((count, width), lambda i: (0, 0)),
            pl.BlockSpec((width, width), lambda i: (0, 0)),
            pl.BlockSpec((width, width), lambda i: (0, 0)),
        ],
        out_specs=pl.BlockSpec((tile, width), lambda i: (i, 0)),
        out_shape=jax.ShapeDtypeStruct((rows, width), BF16),
        scratch_shapes=[pltpu.VMEM((2 * width, 2 * width), BF16)],
        compiler_params=params(),
        cost_estimate=cost(2 * rows * count * width, 8 * rows * width),
        name="grad_y",
    )(own, y, send_rows.reshape(1, count), returned, inverse, spread)


def radices(n):
    result, shift = [], 0
    while 1 << shift < n:
        bits = 1 if shift == 0 else min(2, n.bit_length() - 1 - shift)
        result.append((shift, 1 << bits))
        shift += bits
    return result


def position(relative, n):
    total = 0
    for shift, radix in radices(n):
        total = total * radix + ((relative >> shift) & (radix - 1))
    return total


def backward_kernel(n, x_ref, hidden_ref, slope_ref, gy_ref, w_out_ref, me_ref, *rest):
    *outs, g_in, g_out = rest
    gy = gy_ref[...]
    x = x_ref[...]

    @pl.when(pl.program_id(0) == 0)
    def _():
        g_in[...] = jnp.zeros_like(g_in)
        g_out[...] = jnp.zeros_like(g_out)

    units = g_in.shape[1]
    step = min(512, units)
    for at in range(0, units, step):
        back = dot_nt(gy, w_out_ref[at:at + step, :])
        grad = (back * slope_ref[:, at:at + step].astype(F32)).astype(BF16)
        g_in[:, at:at + step] += dot_tn(x, grad)
    g_out[...] += dot_tn(hidden_ref[...], gy)

    @pl.when(pl.program_id(0) == pl.num_programs(0) - 1)
    def _():
        if n is None:
            outs[0][...] = g_in[...]
            outs[1][...] = g_out[...]
        else:
            me = me_ref[0]
            chunk = g_in.shape[0] // n
            for pair in range(n // 2):
                for side, out in enumerate(outs):
                    c = 2 * pair + (me + side) % 2
                    at = pl.multiple_of((position(me ^ c, n) % (n // 2)) * chunk, chunk)
                    rows = pl.ds(pl.multiple_of(c * chunk, chunk), chunk)
                    out[pl.ds(at, chunk), :units] = g_in[rows, :].astype(out.dtype)
                    out[pl.ds(at, chunk), units:] = g_out[rows, :].astype(out.dtype)


def backward(features, hidden, slope, gy, w_out, me, n):
    nodes, din = features.shape
    units, width = w_out.shape
    tile = min(1024, nodes)
    if n is None:
        outs = [jax.ShapeDtypeStruct((din, units), F32), jax.ShapeDtypeStruct((units, width), F32)]
    else:
        outs = [
            jax.ShapeDtypeStruct((din // 2, units + width), F32),
            jax.ShapeDtypeStruct((din // 2, units + width), BF16),
        ]
    return pl.pallas_call(
        functools.partial(backward_kernel, n),
        grid=(nodes // tile,),
        in_specs=[
            pl.BlockSpec((tile, din), lambda i: (i, 0)),
            pl.BlockSpec((tile, units), lambda i: (i, 0)),
            pl.BlockSpec((tile, units), lambda i: (i, 0)),
            pl.BlockSpec((tile, width), lambda i: (i, 0)),
            pl.BlockSpec((units, width), lambda i: (0, 0)),
            pl.BlockSpec(memory_space=pltpu.SMEM),
        ],
        out_specs=[pl.BlockSpec(o.shape, lambda i: (0, 0)) for o in outs],
        out_shape=outs,
        scratch_shapes=[pltpu.VMEM((din, units), F32), pltpu.VMEM((units, width), F32)],
        compiler_params=params(),
        cost_estimate=cost(2 * nodes * units * (din + 2 * width), 2 * nodes * (din + 2 * units)),
        name="backward",
    )(features, hidden, slope, gy, w_out, me)


def unpack_kernel(n, packed_ref, me_ref, g_in_ref, g_out_ref):
    units = g_in_ref.shape[1]
    rows = g_in_ref.shape[0]
    chunk = packed_ref.shape[0] // n
    me = me_ref[0]
    first = pl.program_id(0) * (rows // chunk)
    for c in range(rows // chunk):
        at = pl.multiple_of(position(me ^ (first + c), n) * chunk, chunk)
        part = packed_ref[pl.ds(at, chunk), :].astype(F32)
        g_in_ref[c * chunk:(c + 1) * chunk, :] = part[:, :units]
        g_out_ref[c * chunk:(c + 1) * chunk, :] = part[:, units:]


def unpack(packed, me, n, width):
    din, both = packed.shape
    units = both - width
    tile = din // 4
    return pl.pallas_call(
        functools.partial(unpack_kernel, n),
        grid=(din // tile,),
        in_specs=[
            pl.BlockSpec((din, both), lambda i: (0, 0)),
            pl.BlockSpec(memory_space=pltpu.SMEM),
        ],
        out_specs=[
            pl.BlockSpec((tile, units), lambda i: (i, 0)),
            pl.BlockSpec((tile, width), lambda i: (i, 0)),
        ],
        out_shape=[
            jax.ShapeDtypeStruct((din, units), F32),
            jax.ShapeDtypeStruct((din, width), F32),
        ],
        compiler_params=params(),
        cost_estimate=cost(din * both, 6 * din * both),
        name="unpack",
    )(packed, me)


def exchange(value, axis, n, mask):
    return lax.ppermute(value, axis, [(i, i ^ mask) for i in range(n)])


def sum_small(value, axis, n, beside):
    if n & (n - 1):
        return lax.psum(value, axis)
    for k, (shift, radix) in enumerate(radices(n)):
        got = [exchange(value, axis, n, m << shift) for m in range(1, radix)]
        if k < len(beside):
            got, _ = lax.optimization_barrier((got, beside[k]))
        value = sum(got, value)
    return value


def reduce_packed(kept, sent, axis, n):
    steps = radices(n)
    value = kept + exchange(sent, axis, n, 1).astype(F32)
    for shift, radix in steps[1:]:
        size = value.shape[0] // radix
        total = value[:size]
        for m in range(1, radix):
            part = value[m * size:(m + 1) * size].astype(BF16)
            total = total + exchange(part, axis, n, m << shift).astype(F32)
        value = total
    value = value.astype(BF16)
    for shift, radix in reversed(steps):
        parts = [value] + [exchange(value, axis, n, m << shift) for m in range(1, radix)]
        value = jnp.concatenate(parts, axis=0)
    return value


def shards(features, w_in, w_out, send_rows, pair_src, pair_weight, pair_mask):
    n_dp = lax.axis_size("dp")
    n_mp = lax.axis_size("mp")
    group_rows, din = features.shape
    nodes = group_rows * n_dp
    rows = group_rows // n_mp
    units, width = w_out.shape
    pairs = pair_src.shape[1]
    count = send_rows.shape[0]
    scale = 1.0 / (pairs * math.sqrt(nodes))
    me = lax.axis_index("dp").astype(jnp.int32).reshape(1)

    per = 256
    src = pair_src.reshape(rows * pairs // per, per)
    coef = (pair_weight * pair_mask.astype(F32)).reshape(rows * pairs // per, per)

    hidden, slope, y = forward(features, w_in, w_out, BF16 if n_mp == 1 else F32)
    if n_mp > 1:
        y = lax.psum_scatter(y, "mp", scatter_dimension=0, tiled=True).astype(BF16)
    sent, gram = send(y, send_rows)
    got = lax.all_to_all(sent, "dp", split_axis=0, concat_axis=0, tiled=True)
    parts = 4 if rows % (4 * 256) == 0 else 1
    weights, scaled, carry, marks = [], [], (), []
    for part in range(parts):
        piece, with_y, *carry = weights_of(src, coef, y, carry, pairs, count, part, parts)
        weights.append(piece)
        scaled.append(with_y)
        marks.append(carry[1])
    gram = sum_small(gram, "dp", n_dp, marks)
    if n_mp > 1:
        gram = lax.psum(gram, "mp")
    back, spread = back_of(got, *carry)
    returned = lax.all_to_all(back, "dp", split_axis=0, concat_axis=0, tiled=True)
    gram, _ = lax.optimization_barrier((gram, back))
    own, inverse = own_of(weights, scaled, got, gram, nodes)
    spread = sum_small(spread, "dp", n_dp, [inverse])
    if n_mp > 1:
        spread = lax.psum(spread, "mp")
    gy = grad_y_of(own, y, send_rows, returned, inverse, spread, nodes, scale)
    if n_mp > 1:
        gy = lax.all_gather(gy, "mp", axis=0, tiled=True)

    packable = n_dp & (n_dp - 1) == 0 and n_dp > 1 and din == units and din % (16 * n_dp) == 0
    if packable:
        kept, given = backward(features, hidden, slope, gy, w_out, me, n_dp)
        return tuple(unpack(reduce_packed(kept, given, "dp", n_dp), me, n_dp, width))
    return lax.psum(tuple(backward(features, hidden, slope, gy, w_out, me, None)), "dp")


def solution(mesh):
    return jax.shard_map(
        shards,
        mesh=mesh,
        in_specs=(
            P("dp", None),
            P(None, "mp"),
            P("mp", None),
            P(("dp", "mp")),
            P(("dp", "mp"), None),
            P(("dp", "mp"), None),
            P(("dp", "mp"), None),
        ),
        out_specs=(P(None, "mp"), P("mp", None)),
        check_vma=False,
    )
```

```python
import functools
import math

import jax
import jax.numpy as jnp
from jax import lax
from jax.experimental import pallas as pl
from jax.experimental.pallas import tpu as pltpu
from jax.sharding import PartitionSpec as P

F32 = jnp.float32
BF16 = jnp.bfloat16
LANES = 128
STEPS = 8
SHIFT = 0.3
VMEM_BYTES = 56 * 1024 * 1024


def params(steps=1):
    return pltpu.CompilerParams(
        dimension_semantics=("arbitrary",) * steps, vmem_limit_bytes=VMEM_BYTES
    )


def cost(flops, read):
    return pl.CostEstimate(flops=int(flops), bytes_accessed=int(read), transcendentals=0)


def dot_tn(a, b):
    return lax.dot_general(a, b, (((0,), (0,)), ((), ())), preferred_element_type=F32)


def dot_nt(a, b):
    return lax.dot_general(a, b, (((1,), (1,)), ((), ())), preferred_element_type=F32)


def dot(a, b):
    return jnp.dot(a, b, preferred_element_type=F32)


def forward_kernel(x_ref, w_in_ref, w_out_ref, hidden_ref, slope_ref, y_ref, round_ref, gram_ref):
    units = w_in_ref.shape[1]
    step = min(512, units)
    x = x_ref[...]
    for at in range(0, units, step):
        pre = dot(x, w_in_ref[:, at:at + step])
        sig = jax.nn.sigmoid(pre)
        act = pre * sig
        hidden_ref[:, at:at + step] = act.astype(BF16)
        slope_ref[:, at:at + step] = sig + act * (1.0 - sig)
    y = dot(hidden_ref[...], w_out_ref[...])
    y_ref[...] = y
    y = y.astype(BF16)
    round_ref[...] = y

    @pl.when(pl.program_id(0) == 0)
    def _():
        gram_ref[...] = jnp.zeros_like(gram_ref)

    gram_ref[...] += dot_tn(y, y)


def forward(features, w_in, w_out):
    nodes, din = features.shape
    units = w_in.shape[1]
    width = w_out.shape[1]
    tile = min(1024, nodes)
    return pl.pallas_call(
        forward_kernel,
        grid=(nodes // tile,),
        in_specs=[
            pl.BlockSpec((tile, din), lambda i: (i, 0)),
            pl.BlockSpec((din, units), lambda i: (0, 0)),
            pl.BlockSpec((units, width), lambda i: (0, 0)),
        ],
        out_specs=[
            pl.BlockSpec((tile, units), lambda i: (i, 0)),
            pl.BlockSpec((tile, units), lambda i: (i, 0)),
            pl.BlockSpec((tile, width), lambda i: (i, 0)),
            pl.BlockSpec((tile, width), lambda i: (i, 0)),
            pl.BlockSpec((width, width), lambda i: (0, 0)),
        ],
        out_shape=[
            jax.ShapeDtypeStruct((nodes, units), BF16),
            jax.ShapeDtypeStruct((nodes, units), F32),
            jax.ShapeDtypeStruct((nodes, width), F32),
            jax.ShapeDtypeStruct((nodes, width), BF16),
            jax.ShapeDtypeStruct((width, width), F32),
        ],
        compiler_params=params(),
        cost_estimate=cost(2 * nodes * units * (din + width), 2 * nodes * (din + 2 * units)),
        name="forward",
    )(features, w_in, w_out)


def send_kernel(index_ref, y_ref, sent_ref, rows_ref):
    some = 16

    @pl.loop(0, sent_ref.shape[0] // some)
    def _(step):
        at = pl.multiple_of(step * some, some)
        for k in range(some):
            rows_ref[pl.ds(at + k, 1), :] = y_ref[pl.ds(index_ref[at + k], 1), :]

    sent_ref[...] = rows_ref[...].astype(BF16)


def send(y, send_rows):
    rows, width = y.shape
    count = send_rows.shape[0]
    return pl.pallas_call(
        send_kernel,
        in_specs=[
            pl.BlockSpec(memory_space=pltpu.SMEM),
            pl.BlockSpec(memory_space=pltpu.VMEM),
        ],
        out_shape=jax.ShapeDtypeStruct((count, width), BF16),
        scratch_shapes=[pltpu.VMEM((count, width), F32)],
        compiler_params=pltpu.CompilerParams(vmem_limit_bytes=VMEM_BYTES),
        cost_estimate=cost(2 * rows * count * width, 2 * width * (rows + count)),
        name="send",
    )(send_rows, y)


def weights_kernel(pairs, first, *refs):
    if first:
        src_ref, coef_ref, y_ref, round_ref, weights_ref, scaled_ref, back_ref, square_ref = refs
    else:
        src_ref, coef_ref, y_ref, round_ref, back_in, square_in = refs[:6]
        weights_ref, scaled_ref, back_ref, square_ref = refs[6:]
    groups, per = src_ref.shape
    count = weights_ref.shape[1]
    members = per // pairs
    high = count // LANES
    held = BF16 if high * members <= 256 else F32

    @pl.when(pl.program_id(0) == 0)
    def _():
        if first:
            back_ref[...] = jnp.zeros_like(back_ref)
            square_ref[...] = jnp.zeros_like(square_ref)
        else:
            back_ref[...] = back_in[...]
            square_ref[...] = square_in[...]

    member = lax.broadcasted_iota(jnp.int32, (1, per), 1) // pairs
    row = lax.broadcasted_iota(jnp.int32, (high * members, per), 0).astype(F32).astype(held)
    lane = lax.broadcasted_iota(jnp.int32, (LANES, per), 0).astype(F32).astype(held)
    src = src_ref[...]
    target = ((src // LANES) * members + member).astype(F32).astype(held)
    low = (src % LANES).astype(F32).astype(held)
    coef = coef_ref[...].astype(BF16).astype(held)
    zero, one = jnp.zeros((), held), jnp.ones((), held)
    for g in range(groups):
        left = jnp.where(row == target[g:g + 1, :], coef[g:g + 1, :], zero).astype(BF16)
        right = jnp.where(lane == low[g:g + 1, :], one, zero).astype(BF16)
        part = dot_nt(left, right).astype(BF16)
        sums = None
        at = slice(g * members, (g + 1) * members)
        for h in range(high):
            piece = part[h * members:(h + 1) * members, :]
            weights_ref[at, h * LANES:(h + 1) * LANES] = piece
            sums = piece.astype(F32) if sums is None else sums + piece.astype(F32)
        scaled_ref[at, :] = jnp.sum(sums, axis=1, keepdims=True) * y_ref[at, :]
    y = round_ref[...]
    left = jnp.concatenate([y.astype(F32).T.astype(BF16), jnp.ones((16, y.shape[0]), BF16)], axis=0)
    back_ref[...] += dot(left, weights_ref[...])
    square_ref[...] += dot_tn(y, scaled_ref[...].astype(BF16))


def weights_of(src, coef, y, rounded, carry, pairs, count, part, parts):
    rows, width = y.shape[0] // parts, y.shape[1]
    per = src.shape[1]
    members = per // pairs
    groups = min(32, src.shape[0] // parts)
    tile = groups * members
    skip = part * (rows // tile)
    sums = [
        jax.ShapeDtypeStruct((width + 16, count), F32),
        jax.ShapeDtypeStruct((width, width), F32),
    ]
    sum_specs = [pl.BlockSpec(x.shape, lambda i: (0, 0)) for x in sums]
    return pl.pallas_call(
        functools.partial(weights_kernel, pairs, part == 0),
        grid=(rows // tile,),
        in_specs=[
            pl.BlockSpec((groups, per), lambda i: (i + skip, 0)),
            pl.BlockSpec((groups, per), lambda i: (i + skip, 0)),
            pl.BlockSpec((tile, width), lambda i: (i + skip, 0)),
            pl.BlockSpec((tile, width), lambda i: (i + skip, 0)),
        ]
        + (sum_specs if part else []),
        out_specs=[
            pl.BlockSpec((tile, count), lambda i: (i, 0)),
            pl.BlockSpec((tile, width), lambda i: (i, 0)),
        ]
        + sum_specs,
        out_shape=[
            jax.ShapeDtypeStruct((rows, count), BF16),
            jax.ShapeDtypeStruct((rows, width), F32),
        ]
        + sums,
        compiler_params=params(),
        cost_estimate=cost(4 * rows * count * width, 2 * rows * count),
        name="weights",
    )(src, coef, y, rounded, *carry)


def back_kernel(shift, got_ref, sums_ref, square_ref, back_ref, spread_ref):
    width = got_ref.shape[1]
    got = got_ref[...]
    sums = sums_ref[...].T
    back = ((sums[:, width:width + 1] - shift) * got.astype(F32) - sums[:, :width]).astype(BF16)
    back_ref[...] = back
    cross = dot(sums_ref[:width, :].astype(BF16), got)
    spread_ref[...] = square_ref[...] - cross + dot_tn(got, back) + shift * dot_tn(got, got)


def back_of(got, sums, square, shift):
    count, width = got.shape
    return pl.pallas_call(
        functools.partial(back_kernel, shift),
        out_shape=[
            jax.ShapeDtypeStruct((count, width), BF16),
            jax.ShapeDtypeStruct((width, width), F32),
        ],
        compiler_params=pltpu.CompilerParams(vmem_limit_bytes=VMEM_BYTES),
        cost_estimate=cost(4 * count * width * width, 6 * count * width),
        name="back",
    )(got, sums, square)


def own_kernel(nodes, part, count, weights_ref, scaled_ref, got_ref, matrix_ref, own_ref, inverse_ref):
    width = inverse_ref.shape[0]
    each = width // STEPS

    @pl.when(pl.program_id(0) == 0)
    def _():
        matrix = matrix_ref[...]
        inverse_ref[...] = matrix * (1.0 / nodes) if part == 0 else matrix

    for step in range(count):

        @pl.when(pl.program_id(0) == step)
        def _():
            own_ref[...] = scaled_ref[...] - dot(weights_ref[...], got_ref[...])
            start = (part * count + step) * each
            inverse_ref[...] = eliminate(inverse_ref[...], start, each)


def eliminate(matrix, start, count, some=4):
    rows = lax.broadcasted_iota(jnp.int32, matrix.shape, 0)
    lanes = lax.broadcasted_iota(jnp.int32, matrix.shape, 1)
    for first in range(start, start + count, some):
        columns = [
            jnp.broadcast_to(matrix[:, k:k + 1], matrix.shape) for k in range(first, first + some)
        ]
        for at, k in enumerate(range(first, first + some)):
            here, column = rows == k, columns[at]
            pivot = 1.0 / column[k:k + 1, :]
            scaled = jnp.where(lanes[:1] == k, pivot, matrix[k:k + 1, :] * pivot)
            rest = jnp.where(lanes == k, 0.0, matrix) - column * scaled
            matrix = jnp.where(here, scaled, rest)
            for later in range(at + 1, some):
                value = columns[later][k:k + 1, :] * pivot
                columns[later] = jnp.where(here, value, columns[later] - column * value)
    return matrix


def own_of(weights, scaled, got, matrix, nodes, part, parts, skip, rows):
    count, width = got.shape
    steps = STEPS // parts
    tile = rows // steps
    return pl.pallas_call(
        functools.partial(own_kernel, nodes, part, steps),
        grid=(steps,),
        in_specs=[
            pl.BlockSpec((tile, count), lambda i: (i + skip // tile, 0)),
            pl.BlockSpec((tile, width), lambda i: (i + skip // tile, 0)),
            pl.BlockSpec((count, width), lambda i: (0, 0)),
            pl.BlockSpec((width, width), lambda i: (0, 0)),
        ],
        out_specs=[
            pl.BlockSpec((tile, width), lambda i: (i, 0)),
            pl.BlockSpec((width, width), lambda i: (0, 0)),
        ],
        out_shape=[
            jax.ShapeDtypeStruct((rows, width), F32),
            jax.ShapeDtypeStruct((width, width), F32),
        ],
        compiler_params=params(),
        cost_estimate=cost(2 * rows * count * width, 2 * rows * count),
        name="own",
    )(weights, scaled, got, matrix)


def split(value):
    first = value.astype(BF16)
    return first, (value - first.astype(F32)).astype(BF16)


def grad_y_kernel(
    nodes, scale, shift, parts, *refs
):
    own_refs = refs[:parts]
    y_ref, index_ref, returned_ref, inverse_ref, spread_ref, out_ref, right_ref = refs[parts:]
    tile, width = y_ref.shape
    count = returned_ref.shape[0]
    each = pl.num_programs(0) // parts

    @pl.when(pl.program_id(0) == 0)
    def _():
        high = lax.Precision.HIGHEST
        inverse = inverse_ref[...]
        half = jnp.dot(inverse, spread_ref[...], precision=high, preferred_element_type=F32)
        sandwich = jnp.dot(half, inverse, precision=high, preferred_element_type=F32)
        for at, value in ((0, 2.0 * scale * inverse), (width, -2.0 * scale / nodes * sandwich)):
            first, second = split(value)
            right_ref[at:at + width, :width] = first
            right_ref[at:at + width, width:] = second

    for part, own_ref in enumerate(own_refs):

        @pl.when(pl.program_id(0) // each == part)
        def _():
            at = lax.broadcasted_iota(jnp.int32, (tile, count), 0) + pl.program_id(0) * tile
            spots = jnp.where(at == index_ref[...], 1.0, 0.0)
            times = jnp.sum(spots, axis=1, keepdims=True)
            y = y_ref[...]
            nearby = own_ref[...] + dot(spots.astype(BF16), returned_ref[...]) + shift * times * y
            first, second = split(nearby)
            y_first, y_second = split(y)
            both = dot(jnp.concatenate([first, y_first], axis=1), right_ref[...])
            rest = dot(jnp.concatenate([second, y_second], axis=1), right_ref[:, :width])
            out_ref[...] = (both[:, :width] + both[:, width:] + rest).astype(BF16)


def part_block(tile, width, part, each):
    return pl.BlockSpec((tile, width), lambda i: (jnp.clip(i - part * each, 0, each - 1), 0))


def grad_y_of(own, y, send_rows, returned, inverse, spread, shift, nodes, scale):
    rows, width = y.shape
    count = returned.shape[0]
    parts = len(own)
    tile = min(512, rows // parts)
    each = rows // tile // parts
    return pl.pallas_call(
        functools.partial(grad_y_kernel, nodes, scale, shift, parts),
        grid=(rows // tile,),
        in_specs=[part_block(tile, width, part, each) for part in range(parts)]
        + [
            pl.BlockSpec((tile, width), lambda i: (i, 0)),
            pl.BlockSpec((1, count), lambda i: (0, 0)),
            pl.BlockSpec((count, width), lambda i: (0, 0)),
            pl.BlockSpec((width, width), lambda i: (0, 0)),
            pl.BlockSpec((width, width), lambda i: (0, 0)),
        ],
        out_specs=pl.BlockSpec((tile, width), lambda i: (i, 0)),
        out_shape=jax.ShapeDtypeStruct((rows, width), BF16),
        scratch_shapes=[pltpu.VMEM((2 * width, 2 * width), BF16)],
        compiler_params=params(),
        cost_estimate=cost(2 * rows * count * width, 8 * rows * width),
        name="grad_y",
    )(*own, y, send_rows.reshape(1, count), returned, inverse, spread)


def radices(n):
    result, shift = [], 0
    while 1 << shift < n:
        bits = 1 if shift == 0 else min(2, n.bit_length() - 1 - shift)
        result.append((shift, 1 << bits))
        shift += bits
    return result


def position(relative, n):
    total = 0
    for shift, radix in radices(n):
        total = total * radix + ((relative >> shift) & (radix - 1))
    return total


def backward_kernel(n, last, x_ref, slope_ref, gy_ref, w_out_ref, me_ref, *rest):
    if last:
        hidden_ref, *outs, g_in, g_out = rest
    else:
        *outs, g_in = rest
        g_out = None
    gy = gy_ref[...]
    x = x_ref[...]

    @pl.when(pl.program_id(0) == 0)
    def _():
        g_in[...] = jnp.zeros_like(g_in)
        if last:
            g_out[...] = jnp.zeros_like(g_out)

    units = g_in.shape[1]
    back = dot_nt(gy, w_out_ref[...])
    grad = (back * slope_ref[...]).astype(BF16)
    g_in[...] += dot_tn(x, grad)
    if last:
        g_out[...] += dot_tn(hidden_ref[...], gy)

    @pl.when(pl.program_id(0) == pl.num_programs(0) - 1)
    def _():
        if n is None:
            outs[0][...] = g_in[...]
            if last:
                outs[1][...] = g_out[...]
        else:
            me = me_ref[0]
            chunk = g_in.shape[0] // n
            for pair in range(n // 2):
                for side, out in enumerate(outs):
                    c = 2 * pair + (me + side) % 2
                    at = pl.multiple_of((position(me ^ c, n) % (n // 2)) * chunk, chunk)
                    rows = pl.ds(pl.multiple_of(c * chunk, chunk), chunk)
                    out[pl.ds(at, chunk), :units] = g_in[rows, :].astype(out.dtype)
                    if last:
                        out[pl.ds(at, chunk), units:] = g_out[rows, :].astype(out.dtype)


def backward(features, hidden, slope, gy, w_out, me, n, part, parts):
    nodes, din = features.shape
    all_units, width = w_out.shape
    units = all_units // parts
    last = part == parts - 1
    tile = min(1024, nodes)
    both = units + width if last else units
    if n is None:
        outs = [jax.ShapeDtypeStruct((din, units), F32)]
        outs += [jax.ShapeDtypeStruct((all_units, width), F32)] if last else []
    else:
        outs = [
            jax.ShapeDtypeStruct((din // 2, both), F32),
            jax.ShapeDtypeStruct((din // 2, both), BF16),
        ]
    return pl.pallas_call(
        functools.partial(backward_kernel, n, last),
        grid=(nodes // tile,),
        in_specs=[
            pl.BlockSpec((tile, din), lambda i: (i, 0)),
            pl.BlockSpec((tile, units), lambda i: (i, part)),
            pl.BlockSpec((tile, width), lambda i: (i, 0)),
            pl.BlockSpec((units, width), lambda i: (part, 0)),
            pl.BlockSpec(memory_space=pltpu.SMEM),
        ]
        + ([pl.BlockSpec((tile, all_units), lambda i: (i, 0))] if last else []),
        out_specs=[pl.BlockSpec(o.shape, lambda i: (0, 0)) for o in outs],
        out_shape=outs,
        scratch_shapes=[pltpu.VMEM((din, units), F32)]
        + ([pltpu.VMEM((all_units, width), F32)] if last else []),
        compiler_params=params(),
        cost_estimate=cost(2 * nodes * units * (din + 2 * width), 2 * nodes * (din + 2 * units)),
        name="backward",
    )(features, slope, gy, w_out, me, *([hidden] if last else []))


def unpack_kernel(n, packed_ref, me_ref, g_in_ref, g_out_ref):
    units = g_in_ref.shape[1]
    rows = g_in_ref.shape[0]
    chunk = packed_ref.shape[0] // n
    me = me_ref[0]
    first = pl.program_id(0) * (rows // chunk)
    for c in range(rows // chunk):
        at = pl.multiple_of(position(me ^ (first + c), n) * chunk, chunk)
        part = packed_ref[pl.ds(at, chunk), :].astype(F32)
        g_in_ref[c * chunk:(c + 1) * chunk, :] = part[:, :units]
        g_out_ref[c * chunk:(c + 1) * chunk, :] = part[:, units:]


def unpack(packed, me, n, width):
    din, both = packed.shape
    units = both - width
    tile = din // 4
    return pl.pallas_call(
        functools.partial(unpack_kernel, n),
        grid=(din // tile,),
        in_specs=[
            pl.BlockSpec((din, both), lambda i: (0, 0)),
            pl.BlockSpec(memory_space=pltpu.SMEM),
        ],
        out_specs=[
            pl.BlockSpec((tile, units), lambda i: (i, 0)),
            pl.BlockSpec((tile, width), lambda i: (i, 0)),
        ],
        out_shape=[
            jax.ShapeDtypeStruct((din, units), F32),
            jax.ShapeDtypeStruct((din, width), F32),
        ],
        compiler_params=params(),
        cost_estimate=cost(din * both, 6 * din * both),
        name="unpack",
    )(packed, me)


def exchange(value, axis, n, mask):
    return lax.ppermute(value, axis, [(i, i ^ mask) for i in range(n)])


def sum_step(value, axis, n, step, after=None):
    if step is None:
        return lax.psum(value, axis)
    shift, radix = step
    got = [exchange(value, axis, n, m << shift) for m in range(1, radix)]
    if after is not None:
        got, _ = lax.optimization_barrier((got, after))
    return sum(got, value)


def reduce_step(value, axis, n, step):
    shift, radix = step
    size = value.shape[0] // radix
    total = value[:size]
    for m in range(1, radix):
        part = value[m * size:(m + 1) * size].astype(BF16)
        total = total + exchange(part, axis, n, m << shift).astype(F32)
    return total


def gather_packed(value, axis, n):
    for shift, radix in reversed(radices(n)):
        parts = [value] + [exchange(value, axis, n, m << shift) for m in range(1, radix)]
        value = jnp.concatenate(parts, axis=0)
    return value


def shards(features, w_in, w_out, send_rows, pair_src, pair_weight, pair_mask):
    n_dp = lax.axis_size("dp")
    n_mp = lax.axis_size("mp")
    group_rows, din = features.shape
    nodes = group_rows * n_dp
    rows = group_rows // n_mp
    units, width = w_out.shape
    pairs = pair_src.shape[1]
    count = send_rows.shape[0]
    scale = 1.0 / (pairs * math.sqrt(nodes))
    me = lax.axis_index("dp").astype(jnp.int32).reshape(1)

    per = 256
    src = pair_src.reshape(rows * pairs // per, per)
    coef = (pair_weight * pair_mask.astype(F32)).reshape(rows * pairs // per, per)

    steps = [None] if n_dp & (n_dp - 1) else radices(n_dp)
    hidden, slope, y, rounded, gram = forward(features, w_in, w_out)
    if n_mp > 1:
        y = lax.psum_scatter(y, "mp", scatter_dimension=0, tiled=True)
        rounded = y.astype(BF16)
        gram = lax.psum(dot_tn(rounded, rounded), "mp")
    sent = send(y, send_rows)
    got = lax.all_to_all(sent, "dp", split_axis=0, concat_axis=0, tiled=True)
    parts = 2 if rows % (2 * 512) == 0 else 1
    weights, scaled, carry = [], [], ()
    for part in range(parts):
        if steps:
            gram = sum_step(gram, "dp", n_dp, steps[0], sent if part == 0 else None)
            steps = steps[1:]
            gram, rounded, carry = lax.optimization_barrier((gram, rounded, carry))
        piece, with_y, *carry = weights_of(
            src, coef, y, rounded, carry, pairs, count, part, parts
        )
        weights.append(piece)
        scaled.append(with_y)
    for step in steps:
        gram = sum_step(gram, "dp", n_dp, step, carry[1])
    gram, carry = lax.optimization_barrier((gram, carry))
    shift = SHIFT * pairs * rows / count
    back, spread = back_of(got, *carry, shift)
    returned = lax.all_to_all(back, "dp", split_axis=0, concat_axis=0, tiled=True)
    matrix, _ = lax.optimization_barrier((gram, back))
    own, marks = [], []
    cuts = 4 if rows % (4 * 256) == 0 else 1
    for cut in range(cuts):
        part, skip = divmod(cut * (rows // cuts), rows // parts)
        piece, matrix = own_of(
            weights[part], scaled[part], got, matrix, nodes, cut, cuts, skip, rows // cuts
        )
        own.append(piece)
        marks.append(matrix)
    steps = [None] if n_dp & (n_dp - 1) else radices(n_dp)
    for k, step in enumerate(steps):
        spread = sum_step(spread, "dp", n_dp, step, marks[min(k, cuts - 1)])
    if n_mp > 1:
        spread = lax.psum(spread, "mp")
    gy = grad_y_of(own, y, send_rows, returned, matrix, spread, shift, nodes, scale)
    if n_mp > 1:
        gy = lax.all_gather(gy, "mp", axis=0, tiled=True)

    packable = n_dp & (n_dp - 1) == 0 and n_dp > 1 and din == units and din % (16 * n_dp) == 0
    if not packable:
        grads = backward(features, hidden, slope, gy, w_out, me, None, 0, 1)
        return lax.psum(tuple(grads), "dp")
    kept, given = backward(features, hidden, slope, gy, w_out, me, n_dp, 0, 1)
    value = kept + exchange(given, "dp", n_dp, 1).astype(F32)
    for step in radices(n_dp)[1:]:
        value = reduce_step(value, "dp", n_dp, step)
    packed = gather_packed(value.astype(BF16), "dp", n_dp)
    return tuple(unpack(packed, me, n_dp, width))


def solution(mesh):
    return jax.shard_map(
        shards,
        mesh=mesh,
        in_specs=(
            P("dp", None),
            P(None, "mp"),
            P("mp", None),
            P(("dp", "mp")),
            P(("dp", "mp"), None),
            P(("dp", "mp"), None),
            P(("dp", "mp"), None),
        ),
        out_specs=(P(None, "mp"), P("mp", None)),
        check_vma=False,
    )
```

```python
import functools
import math

import jax
import jax.numpy as jnp
from jax import lax
from jax.experimental import pallas as pl
from jax.experimental.pallas import tpu as pltpu
from jax.sharding import PartitionSpec as P

F32 = jnp.float32
BF16 = jnp.bfloat16
LANES = 128
STEPS = 8
SHIFT = 0.3
VMEM_BYTES = 56 * 1024 * 1024


def params(steps=1):
    return pltpu.CompilerParams(
        dimension_semantics=("arbitrary",) * steps, vmem_limit_bytes=VMEM_BYTES
    )


def cost(flops, read):
    return pl.CostEstimate(flops=int(flops), bytes_accessed=int(read), transcendentals=0)


def dot_tn(a, b):
    return lax.dot_general(a, b, (((0,), (0,)), ((), ())), preferred_element_type=F32)


def dot_nt(a, b):
    return lax.dot_general(a, b, (((1,), (1,)), ((), ())), preferred_element_type=F32)


def dot(a, b):
    return jnp.dot(a, b, preferred_element_type=F32)


def forward_kernel(x_ref, w_in_ref, w_out_ref, hidden_ref, slope_ref, y_ref, round_ref, gram_ref):
    units = w_in_ref.shape[1]
    step = min(512, units)
    x = x_ref[...]
    for at in range(0, units, step):
        pre = dot(x, w_in_ref[:, at:at + step])
        sig = jax.nn.sigmoid(pre)
        act = pre * sig
        hidden_ref[:, at:at + step] = act.astype(BF16)
        slope_ref[:, at:at + step] = sig + act * (1.0 - sig)
    y = dot(hidden_ref[...], w_out_ref[...])
    y_ref[...] = y
    y = y.astype(BF16)
    round_ref[...] = y

    @pl.when(pl.program_id(0) == 0)
    def _():
        gram_ref[...] = jnp.zeros_like(gram_ref)

    gram_ref[...] += dot_tn(y, y)


def forward(features, w_in, w_out):
    nodes, din = features.shape
    units = w_in.shape[1]
    width = w_out.shape[1]
    tile = min(1024, nodes)
    return pl.pallas_call(
        forward_kernel,
        grid=(nodes // tile,),
        in_specs=[
            pl.BlockSpec((tile, din), lambda i: (i, 0)),
            pl.BlockSpec((din, units), lambda i: (0, 0)),
            pl.BlockSpec((units, width), lambda i: (0, 0)),
        ],
        out_specs=[
            pl.BlockSpec((tile, units), lambda i: (i, 0)),
            pl.BlockSpec((tile, units), lambda i: (i, 0)),
            pl.BlockSpec((tile, width), lambda i: (i, 0)),
            pl.BlockSpec((tile, width), lambda i: (i, 0)),
            pl.BlockSpec((width, width), lambda i: (0, 0)),
        ],
        out_shape=[
            jax.ShapeDtypeStruct((nodes, units), BF16),
            jax.ShapeDtypeStruct((nodes, units), F32),
            jax.ShapeDtypeStruct((nodes, width), F32),
            jax.ShapeDtypeStruct((nodes, width), BF16),
            jax.ShapeDtypeStruct((width, width), F32),
        ],
        compiler_params=params(),
        cost_estimate=cost(2 * nodes * units * (din + width), 2 * nodes * (din + 2 * units)),
        name="forward",
    )(features, w_in, w_out)


def send_kernel(index_ref, y_ref, sent_ref, rows_ref):
    some = 16

    @pl.loop(0, sent_ref.shape[0] // some)
    def _(step):
        at = pl.multiple_of(step * some, some)
        for k in range(some):
            rows_ref[pl.ds(at + k, 1), :] = y_ref[pl.ds(index_ref[at + k], 1), :]

    sent_ref[...] = rows_ref[...].astype(BF16)


def send(y, send_rows):
    rows, width = y.shape
    count = send_rows.shape[0]
    return pl.pallas_call(
        send_kernel,
        in_specs=[
            pl.BlockSpec(memory_space=pltpu.SMEM),
            pl.BlockSpec(memory_space=pltpu.VMEM),
        ],
        out_shape=jax.ShapeDtypeStruct((count, width), BF16),
        scratch_shapes=[pltpu.VMEM((count, width), F32)],
        compiler_params=pltpu.CompilerParams(vmem_limit_bytes=VMEM_BYTES),
        cost_estimate=cost(2 * rows * count * width, 2 * width * (rows + count)),
        name="send",
    )(send_rows, y)


def weights_kernel(pairs, first, *refs):
    if first:
        src_ref, coef_ref, y_ref, round_ref, weights_ref, scaled_ref, back_ref, square_ref = refs
    else:
        src_ref, coef_ref, y_ref, round_ref, back_in, square_in = refs[:6]
        weights_ref, scaled_ref, back_ref, square_ref = refs[6:]
    groups, per = src_ref.shape
    count = weights_ref.shape[1]
    members = per // pairs
    high = count // LANES
    held = BF16 if high * members <= 256 else F32

    @pl.when(pl.program_id(0) == 0)
    def _():
        if first:
            back_ref[...] = jnp.zeros_like(back_ref)
            square_ref[...] = jnp.zeros_like(square_ref)
        else:
            back_ref[...] = back_in[...]
            square_ref[...] = square_in[...]

    member = lax.broadcasted_iota(jnp.int32, (1, per), 1) // pairs
    row = lax.broadcasted_iota(jnp.int32, (high * members, per), 0).astype(F32).astype(held)
    lane = lax.broadcasted_iota(jnp.int32, (LANES, per), 0).astype(F32).astype(held)
    src = src_ref[...]
    target = ((src // LANES) * members + member).astype(F32).astype(held)
    low = (src % LANES).astype(F32).astype(held)
    coef = coef_ref[...].astype(BF16).astype(held)
    zero, one = jnp.zeros((), held), jnp.ones((), held)
    for g in range(groups):
        left = jnp.where(row == target[g:g + 1, :], coef[g:g + 1, :], zero).astype(BF16)
        right = jnp.where(lane == low[g:g + 1, :], one, zero).astype(BF16)
        part = dot_nt(left, right).astype(BF16)
        sums = None
        at = slice(g * members, (g + 1) * members)
        for h in range(high):
            piece = part[h * members:(h + 1) * members, :]
            weights_ref[at, h * LANES:(h + 1) * LANES] = piece
            sums = piece.astype(F32) if sums is None else sums + piece.astype(F32)
        scaled_ref[at, :] = jnp.sum(sums, axis=1, keepdims=True) * y_ref[at, :]
    y = round_ref[...]
    left = jnp.concatenate([y.astype(F32).T.astype(BF16), jnp.ones((16, y.shape[0]), BF16)], axis=0)
    back_ref[...] += dot(left, weights_ref[...])
    square_ref[...] += dot_tn(y, scaled_ref[...].astype(BF16))


def weights_of(src, coef, y, rounded, carry, pairs, count, part, parts):
    rows, width = y.shape[0] // parts, y.shape[1]
    per = src.shape[1]
    members = per // pairs
    groups = min(32, src.shape[0] // parts)
    tile = groups * members
    skip = part * (rows // tile)
    sums = [
        jax.ShapeDtypeStruct((width + 16, count), F32),
        jax.ShapeDtypeStruct((width, width), F32),
    ]
    sum_specs = [pl.BlockSpec(x.shape, lambda i: (0, 0)) for x in sums]
    return pl.pallas_call(
        functools.partial(weights_kernel, pairs, part == 0),
        grid=(rows // tile,),
        in_specs=[
            pl.BlockSpec((groups, per), lambda i: (i + skip, 0)),
            pl.BlockSpec((groups, per), lambda i: (i + skip, 0)),
            pl.BlockSpec((tile, width), lambda i: (i + skip, 0)),
            pl.BlockSpec((tile, width), lambda i: (i + skip, 0)),
        ]
        + (sum_specs if part else []),
        out_specs=[
            pl.BlockSpec((tile, count), lambda i: (i, 0)),
            pl.BlockSpec((tile, width), lambda i: (i, 0)),
        ]
        + sum_specs,
        out_shape=[
            jax.ShapeDtypeStruct((rows, count), BF16),
            jax.ShapeDtypeStruct((rows, width), F32),
        ]
        + sums,
        compiler_params=params(),
        cost_estimate=cost(4 * rows * count * width, 2 * rows * count),
        name="weights",
    )(src, coef, y, rounded, *carry)


def back_kernel(shift, got_ref, sums_ref, square_ref, back_ref, spread_ref):
    width = got_ref.shape[1]
    got = got_ref[...]
    sums = sums_ref[...].T
    back = ((sums[:, width:width + 1] - shift) * got.astype(F32) - sums[:, :width]).astype(BF16)
    back_ref[...] = back
    cross = dot(sums_ref[:width, :].astype(BF16), got)
    spread_ref[...] = square_ref[...] - cross + dot_tn(got, back) + shift * dot_tn(got, got)


def back_of(got, sums, square, shift):
    count, width = got.shape
    return pl.pallas_call(
        functools.partial(back_kernel, shift),
        out_shape=[
            jax.ShapeDtypeStruct((count, width), BF16),
            jax.ShapeDtypeStruct((width, width), F32),
        ],
        compiler_params=pltpu.CompilerParams(vmem_limit_bytes=VMEM_BYTES),
        cost_estimate=cost(4 * count * width * width, 6 * count * width),
        name="back",
    )(got, sums, square)


def own_kernel(nodes, part, count, weights_ref, scaled_ref, got_ref, matrix_ref, own_ref, inverse_ref):
    width = inverse_ref.shape[0]
    each = width // STEPS

    @pl.when(pl.program_id(0) == 0)
    def _():
        matrix = matrix_ref[...]
        inverse_ref[...] = matrix * (1.0 / nodes) if part == 0 else matrix

    for step in range(count):

        @pl.when(pl.program_id(0) == step)
        def _():
            own_ref[...] = scaled_ref[...] - dot(weights_ref[...], got_ref[...])
            start = (part * count + step) * each
            inverse_ref[...] = eliminate(inverse_ref[...], start, each)


def eliminate(matrix, start, count, some=4):
    rows = lax.broadcasted_iota(jnp.int32, matrix.shape, 0)
    lanes = lax.broadcasted_iota(jnp.int32, matrix.shape, 1)
    for first in range(start, start + count, some):
        columns = [
            jnp.broadcast_to(matrix[:, k:k + 1], matrix.shape) for k in range(first, first + some)
        ]
        for at, k in enumerate(range(first, first + some)):
            here, column = rows == k, columns[at]
            pivot = 1.0 / column[k:k + 1, :]
            scaled = jnp.where(lanes[:1] == k, pivot, matrix[k:k + 1, :] * pivot)
            rest = jnp.where(lanes == k, 0.0, matrix) - column * scaled
            matrix = jnp.where(here, scaled, rest)
            for later in range(at + 1, some):
                value = columns[later][k:k + 1, :] * pivot
                columns[later] = jnp.where(here, value, columns[later] - column * value)
    return matrix


def own_of(weights, scaled, got, matrix, nodes, part, parts, skip, rows):
    count, width = got.shape
    steps = STEPS // parts
    tile = rows // steps
    return pl.pallas_call(
        functools.partial(own_kernel, nodes, part, steps),
        grid=(steps,),
        in_specs=[
            pl.BlockSpec((tile, count), lambda i: (i + skip // tile, 0)),
            pl.BlockSpec((tile, width), lambda i: (i + skip // tile, 0)),
            pl.BlockSpec((count, width), lambda i: (0, 0)),
            pl.BlockSpec((width, width), lambda i: (0, 0)),
        ],
        out_specs=[
            pl.BlockSpec((tile, width), lambda i: (i, 0)),
            pl.BlockSpec((width, width), lambda i: (0, 0)),
        ],
        out_shape=[
            jax.ShapeDtypeStruct((rows, width), F32),
            jax.ShapeDtypeStruct((width, width), F32),
        ],
        compiler_params=params(),
        cost_estimate=cost(2 * rows * count * width, 2 * rows * count),
        name="own",
    )(weights, scaled, got, matrix)


def split(value):
    first = value.astype(BF16)
    return first, (value - first.astype(F32)).astype(BF16)


def set_right(nodes, scale, inverse_ref, spread_ref, right_ref):
    width = inverse_ref.shape[0]
    high = lax.Precision.HIGHEST
    inverse = inverse_ref[...]
    half = jnp.dot(inverse, spread_ref[...], precision=high, preferred_element_type=F32)
    sandwich = jnp.dot(half, inverse, precision=high, preferred_element_type=F32)
    for at, value in ((0, 2.0 * scale * inverse), (width, -2.0 * scale / nodes * sandwich)):
        first, second = split(value)
        right_ref[at:at + width, :width] = first
        right_ref[at:at + width, width:] = second


def grad_y_rows(shift, start, own, y, index, returned, right_ref):
    tile, width = y.shape
    at = lax.broadcasted_iota(jnp.int32, (tile, returned.shape[0]), 0) + start
    spots = jnp.where(at == index, 1.0, 0.0)
    times = jnp.sum(spots, axis=1, keepdims=True)
    nearby = own + dot(spots.astype(BF16), returned) + shift * times * y
    first, second = split(nearby)
    y_first, y_second = split(y)
    both = dot(jnp.concatenate([first, y_first], axis=1), right_ref[...])
    rest = dot(jnp.concatenate([second, y_second], axis=1), right_ref[:, :width])
    return (both[:, :width] + both[:, width:] + rest).astype(BF16)


def grad_y_kernel(nodes, scale, shift, parts, *refs):
    own_refs = refs[:parts]
    y_ref, index_ref, returned_ref, inverse_ref, spread_ref, out_ref, right_ref = refs[parts:]
    tile = y_ref.shape[0]
    each = pl.num_programs(0) // parts

    @pl.when(pl.program_id(0) == 0)
    def _():
        set_right(nodes, scale, inverse_ref, spread_ref, right_ref)

    for part, own_ref in enumerate(own_refs):

        @pl.when(pl.program_id(0) // each == part)
        def _():
            out_ref[...] = grad_y_rows(
                shift, pl.program_id(0) * tile, own_ref[...], y_ref[...], index_ref[...],
                returned_ref[...], right_ref
            )


def part_block(tile, width, part, each):
    return pl.BlockSpec((tile, width), lambda i: (jnp.clip(i - part * each, 0, each - 1), 0))


def grad_y_of(own, y, send_rows, returned, inverse, spread, shift, nodes, scale):
    rows, width = y.shape
    count = returned.shape[0]
    parts = len(own)
    tile = min(512, rows // parts)
    each = rows // tile // parts
    return pl.pallas_call(
        functools.partial(grad_y_kernel, nodes, scale, shift, parts),
        grid=(rows // tile,),
        in_specs=[part_block(tile, width, part, each) for part in range(parts)]
        + [
            pl.BlockSpec((tile, width), lambda i: (i, 0)),
            pl.BlockSpec((1, count), lambda i: (0, 0)),
            pl.BlockSpec((count, width), lambda i: (0, 0)),
            pl.BlockSpec((width, width), lambda i: (0, 0)),
            pl.BlockSpec((width, width), lambda i: (0, 0)),
        ],
        out_specs=pl.BlockSpec((tile, width), lambda i: (i, 0)),
        out_shape=jax.ShapeDtypeStruct((rows, width), BF16),
        scratch_shapes=[pltpu.VMEM((2 * width, 2 * width), BF16)],
        compiler_params=params(),
        cost_estimate=cost(2 * rows * count * width, 8 * rows * width),
        name="grad_y",
    )(*own, y, send_rows.reshape(1, count), returned, inverse, spread)


def radices(n):
    result, shift = [], 0
    while 1 << shift < n:
        bits = 1 if shift == 0 else min(2, n.bit_length() - 1 - shift)
        result.append((shift, 1 << bits))
        shift += bits
    return result


def position(relative, n):
    total = 0
    for shift, radix in radices(n):
        total = total * radix + ((relative >> shift) & (radix - 1))
    return total


def add_grads(x_ref, hidden_ref, slope_ref, gy, w_out_ref, g_in, g_out):
    units = g_in.shape[1]
    step = min(512, units)
    x = x_ref[...]
    for at in range(0, units, step):
        back = dot_nt(gy, w_out_ref[at:at + step, :])
        grad = (back * slope_ref[:, at:at + step]).astype(BF16)
        g_in[:, at:at + step] += dot_tn(x, grad)
    g_out[...] += dot_tn(hidden_ref[...], gy)


def backward_kernel(x_ref, hidden_ref, slope_ref, gy_ref, w_out_ref, g_in, g_out):
    @pl.when(pl.program_id(0) == 0)
    def _():
        g_in[...] = jnp.zeros_like(g_in)
        g_out[...] = jnp.zeros_like(g_out)

    add_grads(x_ref, hidden_ref, slope_ref, gy_ref[...], w_out_ref, g_in, g_out)


def backward(features, hidden, slope, gy, w_out):
    nodes, din = features.shape
    units, width = w_out.shape
    tile = min(1024, nodes)
    shapes = [
        jax.ShapeDtypeStruct((din, units), F32),
        jax.ShapeDtypeStruct((units, width), F32),
    ]
    return pl.pallas_call(
        backward_kernel,
        grid=(nodes // tile,),
        in_specs=[
            pl.BlockSpec((tile, din), lambda i: (i, 0)),
            pl.BlockSpec((tile, units), lambda i: (i, 0)),
            pl.BlockSpec((tile, units), lambda i: (i, 0)),
            pl.BlockSpec((tile, width), lambda i: (i, 0)),
            pl.BlockSpec((units, width), lambda i: (0, 0)),
        ],
        out_specs=[pl.BlockSpec(x.shape, lambda i: (0, 0)) for x in shapes],
        out_shape=shapes,
        compiler_params=params(),
        cost_estimate=cost(2 * nodes * units * (din + 2 * width), 2 * nodes * (din + 3 * units)),
        name="backward",
    )(features, hidden, slope, gy, w_out)


def packed_kernel(nodes, scale, shift, n, parts, *refs):
    own_refs = refs[:parts]
    y_ref, index_ref, returned_ref, inverse_ref, spread_ref = refs[parts:parts + 5]
    x_ref, hidden_ref, slope_ref, w_out_ref, me_ref = refs[parts + 5:parts + 10]
    *outs, g_in, g_out, gy_ref, right_ref = refs[parts + 10:]
    tile = y_ref.shape[0]
    some = min(512, tile)
    each = pl.num_programs(0) // parts

    @pl.when(pl.program_id(0) == 0)
    def _():
        set_right(nodes, scale, inverse_ref, spread_ref, right_ref)
        g_in[...] = jnp.zeros_like(g_in)
        g_out[...] = jnp.zeros_like(g_out)

    for part, own_ref in enumerate(own_refs):

        @pl.when(pl.program_id(0) // each == part)
        def _():
            for at in range(0, tile, some):
                gy_ref[at:at + some, :] = grad_y_rows(
                    shift, pl.program_id(0) * tile + at, own_ref[at:at + some, :],
                    y_ref[at:at + some, :], index_ref[...], returned_ref[...], right_ref
                )

    add_grads(x_ref, hidden_ref, slope_ref, gy_ref[...], w_out_ref, g_in, g_out)

    @pl.when(pl.program_id(0) == pl.num_programs(0) - 1)
    def _():
        me = me_ref[0]
        units = g_in.shape[1]
        chunk = g_in.shape[0] // n
        for pair in range(n // 2):
            for side, out in enumerate(outs):
                c = 2 * pair + (me + side) % 2
                at = pl.multiple_of((position(me ^ c, n) % (n // 2)) * chunk, chunk)
                rows = pl.ds(pl.multiple_of(c * chunk, chunk), chunk)
                out[pl.ds(at, chunk), :units] = g_in[rows, :].astype(out.dtype)
                out[pl.ds(at, chunk), units:] = g_out[rows, :].astype(out.dtype)


def packed_grads(
    own, y, send_rows, returned, inverse, spread, features, hidden, slope, w_out, me,
    nodes, scale, shift, n
):
    rows, din = features.shape
    units, width = w_out.shape
    count = returned.shape[0]
    parts = len(own)
    tile = min(1024, rows // parts)
    each = rows // tile // parts
    shapes = [
        jax.ShapeDtypeStruct((din // 2, units + width), F32),
        jax.ShapeDtypeStruct((din // 2, units + width), BF16),
    ]
    return pl.pallas_call(
        functools.partial(packed_kernel, nodes, scale, shift, n, parts),
        grid=(rows // tile,),
        in_specs=[part_block(tile, width, part, each) for part in range(parts)]
        + [
            pl.BlockSpec((tile, width), lambda i: (i, 0)),
            pl.BlockSpec((1, count), lambda i: (0, 0)),
            pl.BlockSpec((count, width), lambda i: (0, 0)),
            pl.BlockSpec((width, width), lambda i: (0, 0)),
            pl.BlockSpec((width, width), lambda i: (0, 0)),
            pl.BlockSpec((tile, din), lambda i: (i, 0)),
            pl.BlockSpec((tile, units), lambda i: (i, 0)),
            pl.BlockSpec((tile, units), lambda i: (i, 0)),
            pl.BlockSpec((units, width), lambda i: (0, 0)),
            pl.BlockSpec(memory_space=pltpu.SMEM),
        ],
        out_specs=[pl.BlockSpec(x.shape, lambda i: (0, 0)) for x in shapes],
        out_shape=shapes,
        scratch_shapes=[
            pltpu.VMEM((din, units), F32),
            pltpu.VMEM((units, width), F32),
            pltpu.VMEM((tile, width), BF16),
            pltpu.VMEM((2 * width, 2 * width), BF16),
        ],
        compiler_params=params(),
        cost_estimate=cost(2 * rows * units * (din + 2 * width), 2 * rows * (din + 3 * units)),
        name="packed_grads",
    )(
        *own, y, send_rows.reshape(1, count), returned, inverse, spread,
        features, hidden, slope, w_out, me
    )


def unpack_kernel(places, lows, me_ref, *refs):
    *pieces, g_in_ref, g_out_ref = refs
    chunk, units = g_in_ref.shape[2:]
    half = len(pieces) // 2
    for k in range(half):

        @pl.when(pl.program_id(0) == k)
        def _():
            for side, piece in enumerate((pieces[k], pieces[half + k])):
                for t, place in enumerate(places):
                    part = piece[t * chunk:(t + 1) * chunk, :].astype(F32)
                    at = place ^ (me_ref[0] // lows)
                    g_in_ref[at, (me_ref[0] + side) % 2] = part[:, :units]
                    g_out_ref[at, (me_ref[0] + side) % 2] = part[:, units:]


def unpack(pieces, spots, places, lows, me, shapes):
    held = pl.BlockSpec(pieces[0].shape, lambda i, *_: (0, 0))

    def spot(i, me_ref):
        value = sum(jnp.where(i == k, x // 2, 0) for k, x in enumerate(spots))
        return 0, value ^ (me_ref[0] % lows // 2), 0, 0

    return pl.pallas_call(
        functools.partial(unpack_kernel, places, lows),
        grid_spec=pltpu.PrefetchScalarGridSpec(
            num_scalar_prefetch=1,
            grid=(len(pieces) // 2,),
            in_specs=[held] * len(pieces),
            out_specs=[pl.BlockSpec((x.shape[0], 2) + x.shape[2:], spot) for x in shapes],
        ),
        out_shape=shapes,
        compiler_params=params(),
        cost_estimate=cost(1e9, 0),
        name="unpack",
    )(me, *pieces)


def exchange(value, axis, n, mask):
    return lax.ppermute(value, axis, [(i, i ^ mask) for i in range(n)])


def sum_step(value, axis, n, step, after=None):
    if step is None:
        return lax.psum(value, axis)
    shift, radix = step
    got = [exchange(value, axis, n, m << shift) for m in range(1, radix)]
    if after is not None:
        got, _ = lax.optimization_barrier((got, after))
    return sum(got, value)


def reduce_step(value, axis, n, step):
    shift, radix = step
    size = value.shape[0] // radix
    total = value[:size]
    for m in range(1, radix):
        part = value[m * size:(m + 1) * size].astype(BF16)
        total = total + exchange(part, axis, n, m << shift).astype(F32)
    return total


def gather_unpack(value, axis, n, me, units):
    steps = radices(n)
    for shift, radix in reversed(steps[2:]):
        parts = [value] + [exchange(value, axis, n, m << shift) for m in range(1, radix)]
        value = jnp.concatenate(parts, axis=0)
    shift, radix = steps[1]
    lows = 2 * radix
    rest = n // lows
    chunk = value.shape[0] // rest
    both = value.shape[1]
    shapes = [
        jax.ShapeDtypeStruct((rest, lows, chunk, size), F32) for size in (units, both - units)
    ]
    places = sorted(range(rest), key=lambda r: position(r * lows, n))
    order = sorted(range(radix), key=lambda m: bin(m).count("1"))
    here = [exchange(value, axis, n, m << shift) if m else value for m in order]
    there = [exchange(piece, axis, n, 1) for piece in here]
    pieces = here + there
    spots = [m << shift for m in order]
    outs = unpack(pieces, spots, places, lows, me, shapes)
    return tuple(x.reshape(n * chunk, -1) for x in outs)


def shards(features, w_in, w_out, send_rows, pair_src, pair_weight, pair_mask):
    n_dp = lax.axis_size("dp")
    n_mp = lax.axis_size("mp")
    group_rows, din = features.shape
    nodes = group_rows * n_dp
    rows = group_rows // n_mp
    units, width = w_out.shape
    pairs = pair_src.shape[1]
    count = send_rows.shape[0]
    scale = 1.0 / (pairs * math.sqrt(nodes))
    me = lax.axis_index("dp").astype(jnp.int32).reshape(1)

    per = 256
    src = pair_src.reshape(rows * pairs // per, per)
    coef = (pair_weight * pair_mask.astype(F32)).reshape(rows * pairs // per, per)

    steps = [None] if n_dp & (n_dp - 1) else radices(n_dp)
    hidden, slope, y, rounded, gram = forward(features, w_in, w_out)
    if n_mp > 1:
        y = lax.psum_scatter(y, "mp", scatter_dimension=0, tiled=True)
        rounded = y.astype(BF16)
        gram = lax.psum(dot_tn(rounded, rounded), "mp")
    sent = send(y, send_rows)
    got = lax.all_to_all(sent, "dp", split_axis=0, concat_axis=0, tiled=True)
    parts = 2 if rows % (2 * 512) == 0 else 1
    weights, scaled, carry = [], [], ()
    for part in range(parts):
        if steps:
            gram = sum_step(gram, "dp", n_dp, steps[0], sent if part == 0 else None)
            steps = steps[1:]
            gram, rounded, carry = lax.optimization_barrier((gram, rounded, carry))
        piece, with_y, *carry = weights_of(
            src, coef, y, rounded, carry, pairs, count, part, parts
        )
        weights.append(piece)
        scaled.append(with_y)
    for step in steps:
        gram = sum_step(gram, "dp", n_dp, step, carry[1])
    gram, carry = lax.optimization_barrier((gram, carry))
    shift = SHIFT * pairs * rows / count
    back, spread = back_of(got, *carry, shift)
    returned = lax.all_to_all(back, "dp", split_axis=0, concat_axis=0, tiled=True)
    matrix, _ = lax.optimization_barrier((gram, back))
    own, marks = [], []
    cuts = 4 if rows % (4 * 256) == 0 else 1
    for cut in range(cuts):
        part, skip = divmod(cut * (rows // cuts), rows // parts)
        piece, matrix = own_of(
            weights[part], scaled[part], got, matrix, nodes, cut, cuts, skip, rows // cuts
        )
        own.append(piece)
        marks.append(matrix)
    steps = [None] if n_dp & (n_dp - 1) else radices(n_dp)
    for k, step in enumerate(steps):
        spread = sum_step(spread, "dp", n_dp, step, marks[min(k, cuts - 1)])
    if n_mp > 1:
        spread = lax.psum(spread, "mp")
    packable = n_dp & (n_dp - 1) == 0 and n_dp > 2 and din == units and din % (16 * n_dp) == 0
    if not packable or n_mp > 1:
        gy = grad_y_of(own, y, send_rows, returned, matrix, spread, shift, nodes, scale)
        if n_mp > 1:
            gy = lax.all_gather(gy, "mp", axis=0, tiled=True)
        return lax.psum(tuple(backward(features, hidden, slope, gy, w_out)), "dp")
    kept, given = packed_grads(
        own, y, send_rows, returned, matrix, spread, features, hidden, slope, w_out, me,
        nodes, scale, shift, n_dp
    )
    value = kept + exchange(given, "dp", n_dp, 1).astype(F32)
    for step in radices(n_dp)[1:]:
        value = reduce_step(value, "dp", n_dp, step)
    return gather_unpack(value.astype(BF16), "dp", n_dp, me, units)


def solution(mesh):
    return jax.shard_map(
        shards,
        mesh=mesh,
        in_specs=(
            P("dp", None),
            P(None, "mp"),
            P("mp", None),
            P(("dp", "mp")),
            P(("dp", "mp"), None),
            P(("dp", "mp"), None),
            P(("dp", "mp"), None),
        ),
        out_specs=(P(None, "mp"), P("mp", None)),
        check_vma=False,
    )
```

```python
import functools
import math

import jax
import jax.numpy as jnp
from jax import lax
from jax.experimental import pallas as pl
from jax.experimental.pallas import tpu as pltpu
from jax.sharding import PartitionSpec as P

F32 = jnp.float32
BF16 = jnp.bfloat16
LANES = 128
STEPS = 8
SHIFT = 0.3
MIB = 1024 * 1024


def params(mib=56):
    return pltpu.CompilerParams(vmem_limit_bytes=mib * MIB)


def cost(flops, read):
    return pl.CostEstimate(flops=int(flops), bytes_accessed=int(read), transcendentals=0)


def dot_tn(a, b):
    return lax.dot_general(a, b, (((0,), (0,)), ((), ())), preferred_element_type=F32)


def dot_nt(a, b):
    return lax.dot_general(a, b, (((1,), (1,)), ((), ())), preferred_element_type=F32)


def dot(a, b):
    return jnp.dot(a, b, preferred_element_type=F32)


def forward_kernel(x_ref, w_in_ref, w_out_ref, hidden_ref, slope_ref, y_ref, round_ref, gram_ref):
    units = w_in_ref.shape[1]
    step = min(512, units)
    x = x_ref[...]
    for at in range(0, units, step):
        pre = dot(x, w_in_ref[:, at:at + step])
        sig = jax.nn.sigmoid(pre)
        act = pre * sig
        hidden_ref[:, at:at + step] = act.astype(BF16)
        slope_ref[:, at:at + step] = sig + act * (1.0 - sig)
    y = dot(hidden_ref[...], w_out_ref[...])
    y_ref[...] = y
    y = y.astype(BF16)
    round_ref[...] = y

    @pl.when(pl.program_id(0) == 0)
    def _():
        gram_ref[...] = jnp.zeros_like(gram_ref)

    gram_ref[...] += dot_tn(y, y)


def forward(features, w_in, w_out):
    nodes, din = features.shape
    units = w_in.shape[1]
    width = w_out.shape[1]
    tile = min(1024, nodes)
    return pl.pallas_call(
        forward_kernel,
        grid=(nodes // tile,),
        in_specs=[
            pl.BlockSpec((tile, din), lambda i: (i, 0)),
            pl.BlockSpec((din, units), lambda i: (0, 0)),
            pl.BlockSpec((units, width), lambda i: (0, 0)),
        ],
        out_specs=[
            pl.BlockSpec((tile, units), lambda i: (i, 0)),
            pl.BlockSpec((tile, units), lambda i: (i, 0)),
            pl.BlockSpec((tile, width), lambda i: (i, 0)),
            pl.BlockSpec((tile, width), lambda i: (i, 0)),
            pl.BlockSpec((width, width), lambda i: (0, 0)),
        ],
        out_shape=[
            jax.ShapeDtypeStruct((nodes, units), BF16),
            jax.ShapeDtypeStruct((nodes, units), F32),
            jax.ShapeDtypeStruct((nodes, width), F32),
            jax.ShapeDtypeStruct((nodes, width), BF16),
            jax.ShapeDtypeStruct((width, width), F32),
        ],
        compiler_params=params(),
        cost_estimate=cost(2 * nodes * units * (din + width), 2 * nodes * (din + 2 * units)),
        name="forward",
    )(features, w_in, w_out)


def send_kernel(index_ref, y_ref, sent_ref, rows_ref):
    some = 16

    @pl.loop(0, sent_ref.shape[0] // some)
    def _(step):
        at = pl.multiple_of(step * some, some)
        for k in range(some):
            rows_ref[pl.ds(at + k, 1), :] = y_ref[pl.ds(index_ref[at + k], 1), :]

    sent_ref[...] = rows_ref[...].astype(BF16)


def send(y, send_rows):
    rows, width = y.shape
    count = send_rows.shape[0]
    return pl.pallas_call(
        send_kernel,
        in_specs=[
            pl.BlockSpec(memory_space=pltpu.SMEM),
            pl.BlockSpec(memory_space=pltpu.VMEM),
        ],
        out_shape=jax.ShapeDtypeStruct((count, width), BF16),
        scratch_shapes=[pltpu.VMEM((count, width), F32)],
        compiler_params=params(),
        cost_estimate=cost(2 * rows * count * width, 2 * width * (rows + count)),
        name="send",
    )(send_rows, y)


def weights_kernel(pairs, first, *refs):
    if first:
        src_ref, coef_ref, y_ref, round_ref, weights_ref, scaled_ref, back_ref, square_ref = refs
    else:
        src_ref, coef_ref, y_ref, round_ref, back_in, square_in = refs[:6]
        weights_ref, scaled_ref, back_ref, square_ref = refs[6:]
    groups, per = src_ref.shape
    count = weights_ref.shape[1]
    members = per // pairs
    high = count // LANES
    held = BF16 if high * members <= 256 else F32

    @pl.when(pl.program_id(0) == 0)
    def _():
        if first:
            back_ref[...] = jnp.zeros_like(back_ref)
            square_ref[...] = jnp.zeros_like(square_ref)
        else:
            back_ref[...] = back_in[...]
            square_ref[...] = square_in[...]

    member = lax.broadcasted_iota(jnp.int32, (1, per), 1) // pairs
    row = lax.broadcasted_iota(jnp.int32, (high * members, per), 0).astype(F32).astype(held)
    lane = lax.broadcasted_iota(jnp.int32, (LANES, per), 0).astype(F32).astype(held)
    src = src_ref[...]
    target = ((src // LANES) * members + member).astype(F32).astype(held)
    low = (src % LANES).astype(F32).astype(held)
    coef = coef_ref[...].astype(BF16).astype(held)
    zero, one = jnp.zeros((), held), jnp.ones((), held)
    for g in range(groups):
        left = jnp.where(row == target[g:g + 1, :], coef[g:g + 1, :], zero).astype(BF16)
        right = jnp.where(lane == low[g:g + 1, :], one, zero).astype(BF16)
        part = dot_nt(left, right).astype(BF16)
        sums = None
        at = slice(g * members, (g + 1) * members)
        for h in range(high):
            piece = part[h * members:(h + 1) * members, :]
            weights_ref[at, h * LANES:(h + 1) * LANES] = piece
            sums = piece.astype(F32) if sums is None else sums + piece.astype(F32)
        scaled_ref[at, :] = jnp.sum(sums, axis=1, keepdims=True) * y_ref[at, :]
    y = round_ref[...]
    left = jnp.concatenate([y.astype(F32).T.astype(BF16), jnp.ones((16, y.shape[0]), BF16)], axis=0)
    back_ref[...] += dot(left, weights_ref[...])
    square_ref[...] += dot_tn(y, scaled_ref[...].astype(BF16))


def weights_of(src, coef, y, rounded, carry, pairs, count, part, parts):
    rows, width = y.shape[0] // parts, y.shape[1]
    per = src.shape[1]
    members = per // pairs
    groups = min(64, src.shape[0] // parts)
    tile = groups * members
    skip = part * (rows // tile)
    sums = [
        jax.ShapeDtypeStruct((width + 16, count), F32),
        jax.ShapeDtypeStruct((width, width), F32),
    ]
    sum_specs = [pl.BlockSpec(x.shape, lambda i: (0, 0)) for x in sums]
    return pl.pallas_call(
        functools.partial(weights_kernel, pairs, part == 0),
        grid=(rows // tile,),
        in_specs=[
            pl.BlockSpec((groups, per), lambda i: (i + skip, 0)),
            pl.BlockSpec((groups, per), lambda i: (i + skip, 0)),
            pl.BlockSpec((tile, width), lambda i: (i + skip, 0)),
            pl.BlockSpec((tile, width), lambda i: (i + skip, 0)),
        ]
        + (sum_specs if part else []),
        out_specs=[
            pl.BlockSpec((tile, count), lambda i: (i, 0)),
            pl.BlockSpec((tile, width), lambda i: (i, 0)),
        ]
        + sum_specs,
        out_shape=[
            jax.ShapeDtypeStruct((rows, count), BF16),
            jax.ShapeDtypeStruct((rows, width), F32),
        ]
        + sums,
        compiler_params=params(),
        cost_estimate=cost(4 * rows * count * width, 2 * rows * count),
        name="weights",
    )(src, coef, y, rounded, *carry)


def back_kernel(shift, got_ref, sums_ref, square_ref, back_ref, spread_ref):
    width = got_ref.shape[1]
    got = got_ref[...]
    sums = sums_ref[...].T
    back = ((sums[:, width:width + 1] - shift) * got.astype(F32) - sums[:, :width]).astype(BF16)
    back_ref[...] = back
    cross = dot(sums_ref[:width, :].astype(BF16), got)
    spread_ref[...] = square_ref[...] - cross + dot_tn(got, back) + shift * dot_tn(got, got)


def back_of(got, sums, square, shift):
    count, width = got.shape
    return pl.pallas_call(
        functools.partial(back_kernel, shift),
        in_specs=[pl.BlockSpec(memory_space=pltpu.VMEM)] * 3,
        out_shape=[
            jax.ShapeDtypeStruct((count, width), BF16),
            jax.ShapeDtypeStruct((width, width), F32),
        ],
        compiler_params=params(),
        cost_estimate=cost(4 * count * width * width, 6 * count * width),
        name="back",
    )(got, sums, square)


def own_kernel(nodes, done, count, weights_ref, scaled_ref, got_ref, matrix_ref, own_ref, inverse_ref):
    width = inverse_ref.shape[0]
    each = width // STEPS

    @pl.when(pl.program_id(0) == 0)
    def _():
        matrix = matrix_ref[...]
        inverse_ref[...] = matrix if done else matrix * (1.0 / nodes)

    for step in range(count):

        @pl.when(pl.program_id(0) == step)
        def _():
            own_ref[...] = scaled_ref[...] - dot(weights_ref[...], got_ref[...])
            start = (done + step) * each
            inverse_ref[...] = eliminate(inverse_ref[...], start, each)


def eliminate(matrix, start, count, some=4):
    rows = lax.broadcasted_iota(jnp.int32, matrix.shape, 0)
    lanes = lax.broadcasted_iota(jnp.int32, matrix.shape, 1)
    for first in range(start, start + count, some):
        columns = [
            jnp.broadcast_to(matrix[:, k:k + 1], matrix.shape) for k in range(first, first + some)
        ]
        for at, k in enumerate(range(first, first + some)):
            here, column = rows == k, columns[at]
            pivot = 1.0 / column[k:k + 1, :]
            scaled = jnp.where(lanes[:1] == k, pivot, matrix[k:k + 1, :] * pivot)
            rest = jnp.where(lanes == k, 0.0, matrix) - column * scaled
            matrix = jnp.where(here, scaled, rest)
            for later in range(at + 1, some):
                value = columns[later][k:k + 1, :] * pivot
                columns[later] = jnp.where(here, value, columns[later] - column * value)
    return matrix


def own_of(weights, scaled, got, matrix, nodes, done, steps, skip, tile):
    count, width = got.shape
    rows = steps * tile
    return pl.pallas_call(
        functools.partial(own_kernel, nodes, done, steps),
        grid=(steps,),
        in_specs=[
            pl.BlockSpec((tile, count), lambda i: (i + skip, 0)),
            pl.BlockSpec((tile, width), lambda i: (i + skip, 0)),
            pl.BlockSpec(memory_space=pltpu.VMEM),
            pl.BlockSpec((width, width), lambda i: (0, 0)),
        ],
        out_specs=[
            pl.BlockSpec((tile, width), lambda i: (i, 0)),
            pl.BlockSpec((width, width), lambda i: (0, 0)),
        ],
        out_shape=[
            jax.ShapeDtypeStruct((rows, width), F32),
            jax.ShapeDtypeStruct((width, width), F32),
        ],
        compiler_params=params(),
        cost_estimate=cost(2 * rows * count * width, 2 * rows * count),
        name="own",
    )(weights, scaled, got, matrix)


def split(value):
    first = value.astype(BF16)
    return first, (value - first.astype(F32)).astype(BF16)


def set_right(nodes, scale, inverse_ref, spread_ref, right_ref):
    width = inverse_ref.shape[0]
    high = lax.Precision.HIGHEST
    inverse = inverse_ref[...]
    half = jnp.dot(inverse, spread_ref[...], precision=high, preferred_element_type=F32)
    sandwich = jnp.dot(half, inverse, precision=high, preferred_element_type=F32)
    for at, value in ((0, 2.0 * scale * inverse), (width, -2.0 * scale / nodes * sandwich)):
        first, second = split(value)
        right_ref[at:at + width, :width] = first
        right_ref[at:at + width, width:] = second


def grad_y_rows(shift, start, own, y, index, returned, right_ref):
    tile, width = y.shape
    at = lax.broadcasted_iota(jnp.int32, (tile, returned.shape[0]), 0) + start
    spots = jnp.where(at == index, 1.0, 0.0)
    times = jnp.sum(spots, axis=1, keepdims=True)
    nearby = own + dot(spots.astype(BF16), returned) + shift * times * y
    first, second = split(nearby)
    y_first, y_second = split(y)
    both = dot(jnp.concatenate([first, y_first], axis=1), right_ref[...])
    rest = dot(jnp.concatenate([second, y_second], axis=1), right_ref[:, :width])
    return (both[:, :width] + both[:, width:] + rest).astype(BF16)


def grad_y_kernel(nodes, scale, shift, places, *refs):
    parts = len(places)
    own_refs = refs[:parts]
    y_ref, index_ref, returned_ref, inverse_ref, spread_ref, out_ref, right_ref = refs[parts:]
    tile = y_ref.shape[0]

    @pl.when(pl.program_id(0) == 0)
    def _():
        set_right(nodes, scale, inverse_ref, spread_ref, right_ref)

    for place, own_ref in zip(places, own_refs):

        @pl.when(in_span(*place))
        def _():
            out_ref[...] = grad_y_rows(
                shift, pl.program_id(0) * tile, own_ref[...], y_ref[...], index_ref[...],
                returned_ref[...], right_ref
            )


def spans(arrays, tile):
    result, first = [], 0
    for x in arrays:
        result.append((first, x.shape[0] // tile))
        first += x.shape[0] // tile
    return result


def span_block(tile, width, first, each):
    return pl.BlockSpec((tile, width), lambda i: (jnp.clip(i - first, 0, each - 1), 0))


def in_span(first, each):
    return (pl.program_id(0) >= first) & (pl.program_id(0) < first + each)


def grad_y_of(own, y, send_rows, returned, inverse, spread, shift, nodes, scale):
    rows, width = y.shape
    count = returned.shape[0]
    tile = min(512, own[0].shape[0])
    places = spans(own, tile)
    return pl.pallas_call(
        functools.partial(grad_y_kernel, nodes, scale, shift, places),
        grid=(rows // tile,),
        in_specs=[span_block(tile, width, *place) for place in places]
        + [
            pl.BlockSpec((tile, width), lambda i: (i, 0)),
            pl.BlockSpec((1, count), lambda i: (0, 0)),
            pl.BlockSpec((count, width), lambda i: (0, 0)),
            pl.BlockSpec((width, width), lambda i: (0, 0)),
            pl.BlockSpec((width, width), lambda i: (0, 0)),
        ],
        out_specs=pl.BlockSpec((tile, width), lambda i: (i, 0)),
        out_shape=jax.ShapeDtypeStruct((rows, width), BF16),
        scratch_shapes=[pltpu.VMEM((2 * width, 2 * width), BF16)],
        compiler_params=params(),
        cost_estimate=cost(2 * rows * count * width, 8 * rows * width),
        name="grad_y",
    )(*own, y, send_rows.reshape(1, count), returned, inverse, spread)


def radices(n):
    result, shift = [], 0
    while 1 << shift < n:
        bits = 1 if shift == 0 else min(2, n.bit_length() - 1 - shift)
        result.append((shift, 1 << bits))
        shift += bits
    return result


def position(relative, n):
    total = 0
    for shift, radix in radices(n):
        total = total * radix + ((relative >> shift) & (radix - 1))
    return total


def add_grads(x_ref, hidden_ref, slope_ref, gy, w_out_ref, g_in, g_out):
    units = g_in.shape[1]
    step = min(512, units)
    x = x_ref[...]
    for at in range(0, units, step):
        back = dot_nt(gy, w_out_ref[at:at + step, :])
        grad = (back * slope_ref[:, at:at + step]).astype(BF16)
        g_in[:, at:at + step] += dot_tn(x, grad)
    g_out[...] += dot_tn(hidden_ref[...], gy)


def backward_kernel(x_ref, hidden_ref, slope_ref, gy_ref, w_out_ref, g_in, g_out):
    @pl.when(pl.program_id(0) == 0)
    def _():
        g_in[...] = jnp.zeros_like(g_in)
        g_out[...] = jnp.zeros_like(g_out)

    add_grads(x_ref, hidden_ref, slope_ref, gy_ref[...], w_out_ref, g_in, g_out)


def backward(features, hidden, slope, gy, w_out):
    nodes, din = features.shape
    units, width = w_out.shape
    tile = min(1024, nodes)
    shapes = [
        jax.ShapeDtypeStruct((din, units), F32),
        jax.ShapeDtypeStruct((units, width), F32),
    ]
    return pl.pallas_call(
        backward_kernel,
        grid=(nodes // tile,),
        in_specs=[
            pl.BlockSpec((tile, din), lambda i: (i, 0)),
            pl.BlockSpec((tile, units), lambda i: (i, 0)),
            pl.BlockSpec((tile, units), lambda i: (i, 0)),
            pl.BlockSpec((tile, width), lambda i: (i, 0)),
            pl.BlockSpec((units, width), lambda i: (0, 0)),
        ],
        out_specs=[pl.BlockSpec(x.shape, lambda i: (0, 0)) for x in shapes],
        out_shape=shapes,
        compiler_params=params(),
        cost_estimate=cost(2 * nodes * units * (din + 2 * width), 2 * nodes * (din + 3 * units)),
        name="backward",
    )(features, hidden, slope, gy, w_out)


def packed_kernel(nodes, scale, shift, n, places, *refs):
    parts = len(places)
    own_refs = refs[:parts]
    y_ref, index_ref, returned_ref, inverse_ref, spread_ref = refs[parts:parts + 5]
    x_ref, hidden_ref, slope_ref, w_out_ref, me_ref = refs[parts + 5:parts + 10]
    *outs, g_in, g_out, gy_ref, right_ref = refs[parts + 10:]
    tile = y_ref.shape[0]
    some = min(512, tile)

    @pl.when(pl.program_id(0) == 0)
    def _():
        set_right(nodes, scale, inverse_ref, spread_ref, right_ref)
        g_in[...] = jnp.zeros_like(g_in)
        g_out[...] = jnp.zeros_like(g_out)

    for place, own_ref in zip(places, own_refs):

        @pl.when(in_span(*place))
        def _():
            for at in range(0, tile, some):
                gy_ref[at:at + some, :] = grad_y_rows(
                    shift, pl.program_id(0) * tile + at, own_ref[at:at + some, :],
                    y_ref[at:at + some, :], index_ref[...], returned_ref[...], right_ref
                )

    add_grads(x_ref, hidden_ref, slope_ref, gy_ref[...], w_out_ref, g_in, g_out)

    @pl.when(pl.program_id(0) == pl.num_programs(0) - 1)
    def _():
        me = me_ref[0]
        units = g_in.shape[1]
        chunk = g_in.shape[0] // n
        for pair in range(n // 2):
            for side, out in enumerate(outs):
                c = 2 * pair + (me + side) % 2
                at = pl.multiple_of((position(me ^ c, n) % (n // 2)) * chunk, chunk)
                rows = pl.ds(pl.multiple_of(c * chunk, chunk), chunk)
                out[pl.ds(at, chunk), :units] = g_in[rows, :].astype(out.dtype)
                out[pl.ds(at, chunk), units:] = g_out[rows, :].astype(out.dtype)


def packed_grads(
    own, y, send_rows, returned, inverse, spread, features, hidden, slope, w_out, me,
    nodes, scale, shift, n
):
    rows, din = features.shape
    units, width = w_out.shape
    count = returned.shape[0]
    tile = min(1024, own[0].shape[0])
    places = spans(own, tile)
    shapes = [
        jax.ShapeDtypeStruct((din // 2, units + width), F32),
        jax.ShapeDtypeStruct((din // 2, units + width), BF16),
    ]
    return pl.pallas_call(
        functools.partial(packed_kernel, nodes, scale, shift, n, places),
        grid=(rows // tile,),
        in_specs=[span_block(tile, width, *place) for place in places]
        + [
            pl.BlockSpec((tile, width), lambda i: (i, 0)),
            pl.BlockSpec((1, count), lambda i: (0, 0)),
            pl.BlockSpec(memory_space=pltpu.VMEM),
            pl.BlockSpec((width, width), lambda i: (0, 0)),
            pl.BlockSpec((width, width), lambda i: (0, 0)),
            pl.BlockSpec((tile, din), lambda i: (i, 0)),
            pl.BlockSpec((tile, units), lambda i: (i, 0)),
            pl.BlockSpec((tile, units), lambda i: (i, 0)),
            pl.BlockSpec((units, width), lambda i: (0, 0)),
            pl.BlockSpec(memory_space=pltpu.SMEM),
        ],
        out_specs=[pl.BlockSpec(x.shape, lambda i: (0, 0)) for x in shapes],
        out_shape=shapes,
        scratch_shapes=[
            pltpu.VMEM((din, units), F32),
            pltpu.VMEM((units, width), F32),
            pltpu.VMEM((tile, width), BF16),
            pltpu.VMEM((2 * width, 2 * width), BF16),
        ],
        compiler_params=params(50),
        cost_estimate=cost(2 * rows * units * (din + 2 * width), 2 * rows * (din + 3 * units)),
        name="packed_grads",
    )(
        *own, y, send_rows.reshape(1, count), returned, inverse, spread,
        features, hidden, slope, w_out, me
    )


def unpack_kernel(places, lows, me_ref, *refs):
    *pieces, g_in_ref, g_out_ref = refs
    chunk, units = g_in_ref.shape[2:]
    half = len(pieces) // 2
    for k in range(half):

        @pl.when(pl.program_id(0) == k)
        def _():
            for side, piece in enumerate((pieces[k], pieces[half + k])):
                for t, place in enumerate(places):
                    part = piece[t * chunk:(t + 1) * chunk, :].astype(F32)
                    at = place ^ (me_ref[0] // lows)
                    g_in_ref[at, (me_ref[0] + side) % 2] = part[:, :units]
                    g_out_ref[at, (me_ref[0] + side) % 2] = part[:, units:]


def unpack(pieces, spots, places, lows, me, shapes):
    held = pl.BlockSpec(memory_space=pltpu.VMEM)

    def spot(i, me_ref):
        value = sum(jnp.where(i == k, x // 2, 0) for k, x in enumerate(spots))
        return 0, value ^ (me_ref[0] % lows // 2), 0, 0

    return pl.pallas_call(
        functools.partial(unpack_kernel, places, lows),
        grid_spec=pltpu.PrefetchScalarGridSpec(
            num_scalar_prefetch=1,
            grid=(len(pieces) // 2,),
            in_specs=[held] * len(pieces),
            out_specs=[pl.BlockSpec((x.shape[0], 2) + x.shape[2:], spot) for x in shapes],
        ),
        out_shape=shapes,
        compiler_params=params(12),
        cost_estimate=cost(1e9, 0),
        name="unpack",
    )(me, *pieces)


def exchange(value, axis, n, mask):
    return lax.ppermute(value, axis, [(i, i ^ mask) for i in range(n)])


def sum_step(value, axis, n, step, after=None):
    if step is None:
        return lax.psum(value, axis)
    shift, radix = step
    got = [exchange(value, axis, n, m << shift) for m in range(1, radix)]
    if after is not None:
        got, _ = lax.optimization_barrier((got, after))
    return sum(got, value)


def reduce_step(value, axis, n, step):
    shift, radix = step
    size = value.shape[0] // radix
    total = value[:size]
    for m in range(1, radix):
        part = value[m * size:(m + 1) * size].astype(BF16)
        total = total + exchange(part, axis, n, m << shift).astype(F32)
    return total


def gather_unpack(value, axis, n, me, units):
    steps = radices(n)
    for shift, radix in reversed(steps[2:]):
        parts = [value] + [exchange(value, axis, n, m << shift) for m in range(1, radix)]
        value = jnp.concatenate(parts, axis=0)
    shift, radix = steps[1]
    lows = 2 * radix
    rest = n // lows
    chunk = value.shape[0] // rest
    both = value.shape[1]
    shapes = [
        jax.ShapeDtypeStruct((rest, lows, chunk, size), F32) for size in (units, both - units)
    ]
    places = sorted(range(rest), key=lambda r: position(r * lows, n))
    order = sorted(range(radix), key=lambda m: bin(m).count("1"))
    here = [exchange(value, axis, n, m << shift) if m else value for m in order]
    there = [exchange(piece, axis, n, 1) for piece in here]
    pieces = here + there
    spots = [m << shift for m in order]
    outs = unpack(pieces, spots, places, lows, me, shapes)
    return tuple(x.reshape(n * chunk, -1) for x in outs)


def shards(features, w_in, w_out, send_rows, pair_src, pair_weight, pair_mask):
    n_dp = lax.axis_size("dp")
    n_mp = lax.axis_size("mp")
    group_rows, din = features.shape
    nodes = group_rows * n_dp
    rows = group_rows // n_mp
    units, width = w_out.shape
    pairs = pair_src.shape[1]
    count = send_rows.shape[0]
    scale = 1.0 / (pairs * math.sqrt(nodes))
    me = lax.axis_index("dp").astype(jnp.int32).reshape(1)

    per = 256
    src = pair_src.reshape(rows * pairs // per, per)
    coef = (pair_weight * pair_mask.astype(F32)).reshape(rows * pairs // per, per)

    steps = [None] if n_dp & (n_dp - 1) else radices(n_dp)
    hidden, slope, y, rounded, gram = forward(features, w_in, w_out)
    if n_mp > 1:
        y = lax.psum_scatter(y, "mp", scatter_dimension=0, tiled=True)
        rounded = y.astype(BF16)
        gram = lax.psum(dot_tn(rounded, rounded), "mp")
    sent = send(y, send_rows)
    got = lax.all_to_all(sent, "dp", split_axis=0, concat_axis=0, tiled=True)
    parts = 2 if rows % (2 * 512) == 0 else 1
    weights, scaled, carry = [], [], ()
    for part in range(parts):
        if steps:
            gram = sum_step(gram, "dp", n_dp, steps[0], sent if part == 0 else None)
            steps = steps[1:]
            gram, rounded, carry = lax.optimization_barrier((gram, rounded, carry))
        piece, with_y, *carry = weights_of(
            src, coef, y, rounded, carry, pairs, count, part, parts
        )
        weights.append(piece)
        scaled.append(with_y)
    for step in steps:
        gram = sum_step(gram, "dp", n_dp, step, carry[1])
    gram, carry = lax.optimization_barrier((gram, carry))
    shift = SHIFT * pairs * rows / count
    back, spread = back_of(got, *carry, shift)
    returned = lax.all_to_all(back, "dp", split_axis=0, concat_axis=0, tiled=True)
    matrix, _ = lax.optimization_barrier((gram, back))
    own, marks = [], []
    half = STEPS // parts
    cuts = [(0, 2), (2, 2), (4, 4)] if parts == 2 else [(0, STEPS)]
    for done, taken in cuts:
        part, skip = divmod(done, half)
        piece, matrix = own_of(
            weights[part], scaled[part], got, matrix, nodes, done, taken, skip, rows // STEPS
        )
        own.append(piece)
        marks.append(matrix)
    steps = [None] if n_dp & (n_dp - 1) else radices(n_dp)
    for k, step in enumerate(steps):
        spread = sum_step(spread, "dp", n_dp, step, marks[min(k, len(marks) - 1)])
    if n_mp > 1:
        spread = lax.psum(spread, "mp")
    packable = n_dp & (n_dp - 1) == 0 and n_dp > 2 and din == units and din % (16 * n_dp) == 0
    if not packable or n_mp > 1:
        gy = grad_y_of(own, y, send_rows, returned, matrix, spread, shift, nodes, scale)
        if n_mp > 1:
            gy = lax.all_gather(gy, "mp", axis=0, tiled=True)
        return lax.psum(tuple(backward(features, hidden, slope, gy, w_out)), "dp")
    kept, given = packed_grads(
        own, y, send_rows, returned, matrix, spread, features, hidden, slope, w_out, me,
        nodes, scale, shift, n_dp
    )
    value = kept + exchange(given, "dp", n_dp, 1).astype(F32)
    for step in radices(n_dp)[1:]:
        value = reduce_step(value, "dp", n_dp, step)
    return gather_unpack(value.astype(BF16), "dp", n_dp, me, units)


def solution(mesh):
    return jax.shard_map(
        shards,
        mesh=mesh,
        in_specs=(
            P("dp", None),
            P(None, "mp"),
            P("mp", None),
            P(("dp", "mp")),
            P(("dp", "mp"), None),
            P(("dp", "mp"), None),
            P(("dp", "mp"), None),
        ),
        out_specs=(P(None, "mp"), P("mp", None)),
        check_vma=False,
    )
```

```python
import functools
import math

import jax
import jax.numpy as jnp
from jax import lax
from jax.experimental import pallas as pl
from jax.experimental.pallas import tpu as pltpu
from jax.sharding import PartitionSpec as P

F32 = jnp.float32
BF16 = jnp.bfloat16
LANES = 128
STEPS = 4
SHIFT = 0.3
MIB = 1024 * 1024


def params(mib=56):
    return pltpu.CompilerParams(vmem_limit_bytes=mib * MIB)


def cost(flops, read):
    return pl.CostEstimate(flops=int(flops), bytes_accessed=int(read), transcendentals=0)


def dot_tn(a, b):
    return lax.dot_general(a, b, (((0,), (0,)), ((), ())), preferred_element_type=F32)


def dot_nt(a, b):
    return lax.dot_general(a, b, (((1,), (1,)), ((), ())), preferred_element_type=F32)


def dot(a, b):
    return jnp.dot(a, b, preferred_element_type=F32)


def forward_kernel(x_ref, w_in_ref, w_out_ref, hidden_ref, slope_ref, y_ref, round_ref, gram_ref):
    units = w_in_ref.shape[1]
    step = min(512, units)
    x = x_ref[...]
    for at in range(0, units, step):
        pre = dot(x, w_in_ref[:, at:at + step])
        sig = jax.nn.sigmoid(pre)
        act = pre * sig
        hidden_ref[:, at:at + step] = act.astype(BF16)
        slope_ref[:, at:at + step] = sig + act * (1.0 - sig)
    y = dot(hidden_ref[...], w_out_ref[...])
    y_ref[...] = y
    y = y.astype(BF16)
    round_ref[...] = y

    @pl.when(pl.program_id(0) == 0)
    def _():
        gram_ref[...] = jnp.zeros_like(gram_ref)

    gram_ref[...] += dot_tn(y, y)


def forward(features, w_in, w_out):
    nodes, din = features.shape
    units = w_in.shape[1]
    width = w_out.shape[1]
    tile = min(1024, nodes)
    return pl.pallas_call(
        forward_kernel,
        grid=(nodes // tile,),
        in_specs=[
            pl.BlockSpec((tile, din), lambda i: (i, 0)),
            pl.BlockSpec((din, units), lambda i: (0, 0)),
            pl.BlockSpec((units, width), lambda i: (0, 0)),
        ],
        out_specs=[
            pl.BlockSpec((tile, units), lambda i: (i, 0)),
            pl.BlockSpec((tile, units), lambda i: (i, 0)),
            pl.BlockSpec((tile, width), lambda i: (i, 0)),
            pl.BlockSpec((tile, width), lambda i: (i, 0)),
            pl.BlockSpec((width, width), lambda i: (0, 0)),
        ],
        out_shape=[
            jax.ShapeDtypeStruct((nodes, units), BF16),
            jax.ShapeDtypeStruct((nodes, units), F32),
            jax.ShapeDtypeStruct((nodes, width), F32),
            jax.ShapeDtypeStruct((nodes, width), BF16),
            jax.ShapeDtypeStruct((width, width), F32),
        ],
        compiler_params=params(),
        cost_estimate=cost(2 * nodes * units * (din + width), 2 * nodes * (din + 2 * units)),
        name="forward",
    )(features, w_in, w_out)


def send_kernel(index_ref, y_ref, sent_ref, rows_ref):
    some = 16

    @pl.loop(0, sent_ref.shape[0] // some)
    def _(step):
        at = pl.multiple_of(step * some, some)
        for k in range(some):
            rows_ref[pl.ds(at + k, 1), :] = y_ref[pl.ds(index_ref[at + k], 1), :]

    sent_ref[...] = rows_ref[...].astype(BF16)


def send(y, send_rows):
    rows, width = y.shape
    count = send_rows.shape[0]
    return pl.pallas_call(
        send_kernel,
        in_specs=[
            pl.BlockSpec(memory_space=pltpu.SMEM),
            pl.BlockSpec(memory_space=pltpu.VMEM),
        ],
        out_shape=jax.ShapeDtypeStruct((count, width), BF16),
        scratch_shapes=[pltpu.VMEM((count, width), F32)],
        compiler_params=params(),
        cost_estimate=cost(2 * rows * count * width, 2 * width * (rows + count)),
        name="send",
    )(send_rows, y)


def weights_kernel(pairs, first, *refs):
    if first:
        src_ref, coef_ref, y_ref, round_ref, weights_ref, scaled_ref, back_ref, square_ref = refs
    else:
        src_ref, coef_ref, y_ref, round_ref, back_in, square_in = refs[:6]
        weights_ref, scaled_ref, back_ref, square_ref = refs[6:]
    groups, per = src_ref.shape
    count = weights_ref.shape[1]
    members = per // pairs
    high = count // LANES
    held = BF16 if high * members <= 256 else F32

    @pl.when(pl.program_id(0) == 0)
    def _():
        if first:
            back_ref[...] = jnp.zeros_like(back_ref)
            square_ref[...] = jnp.zeros_like(square_ref)
        else:
            back_ref[...] = back_in[...]
            square_ref[...] = square_in[...]

    member = lax.broadcasted_iota(jnp.int32, (1, per), 1) // pairs
    row = lax.broadcasted_iota(jnp.int32, (high * members, per), 0).astype(F32).astype(held)
    lane = lax.broadcasted_iota(jnp.int32, (LANES, per), 0).astype(F32).astype(held)
    src = src_ref[...]
    target = ((src // LANES) * members + member).astype(F32).astype(held)
    low = (src % LANES).astype(F32).astype(held)
    coef = coef_ref[...].astype(BF16).astype(held)
    zero, one = jnp.zeros((), held), jnp.ones((), held)
    for g in range(groups):
        left = jnp.where(row == target[g:g + 1, :], coef[g:g + 1, :], zero).astype(BF16)
        right = jnp.where(lane == low[g:g + 1, :], one, zero).astype(BF16)
        part = dot_nt(left, right).astype(BF16)
        sums = None
        at = slice(g * members, (g + 1) * members)
        for h in range(high):
            piece = part[h * members:(h + 1) * members, :]
            weights_ref[at, h * LANES:(h + 1) * LANES] = piece
            sums = piece.astype(F32) if sums is None else sums + piece.astype(F32)
        scaled_ref[at, :] = jnp.sum(sums, axis=1, keepdims=True) * y_ref[at, :]
    y = round_ref[...]
    left = jnp.concatenate([y.astype(F32).T.astype(BF16), jnp.ones((16, y.shape[0]), BF16)], axis=0)
    back_ref[...] += dot(left, weights_ref[...])
    square_ref[...] += dot_tn(y, scaled_ref[...].astype(BF16))


def weights_of(src, coef, y, rounded, carry, pairs, count, part, parts):
    rows, width = y.shape[0] // parts, y.shape[1]
    per = src.shape[1]
    members = per // pairs
    groups = min(64, src.shape[0] // parts)
    tile = groups * members
    skip = part * (rows // tile)
    sums = [
        jax.ShapeDtypeStruct((width + 16, count), F32),
        jax.ShapeDtypeStruct((width, width), F32),
    ]
    sum_specs = [pl.BlockSpec(x.shape, lambda i: (0, 0)) for x in sums]
    return pl.pallas_call(
        functools.partial(weights_kernel, pairs, part == 0),
        grid=(rows // tile,),
        in_specs=[
            pl.BlockSpec((groups, per), lambda i: (i + skip, 0)),
            pl.BlockSpec((groups, per), lambda i: (i + skip, 0)),
            pl.BlockSpec((tile, width), lambda i: (i + skip, 0)),
            pl.BlockSpec((tile, width), lambda i: (i + skip, 0)),
        ]
        + (sum_specs if part else []),
        out_specs=[
            pl.BlockSpec((tile, count), lambda i: (i, 0)),
            pl.BlockSpec((tile, width), lambda i: (i, 0)),
        ]
        + sum_specs,
        out_shape=[
            jax.ShapeDtypeStruct((rows, count), BF16),
            jax.ShapeDtypeStruct((rows, width), F32),
        ]
        + sums,
        compiler_params=params(),
        cost_estimate=cost(4 * rows * count * width, 2 * rows * count),
        name="weights",
    )(src, coef, y, rounded, *carry)


def back_kernel(shift, got_ref, sums_ref, square_ref, back_ref, spread_ref):
    width = got_ref.shape[1]
    got = got_ref[...]
    sums = sums_ref[...].T
    back = ((sums[:, width:width + 1] - shift) * got.astype(F32) - sums[:, :width]).astype(BF16)
    back_ref[...] = back
    cross = dot(sums_ref[:width, :].astype(BF16), got)
    spread_ref[...] = square_ref[...] - cross + dot_tn(got, back) + shift * dot_tn(got, got)


def back_of(got, sums, square, shift):
    count, width = got.shape
    return pl.pallas_call(
        functools.partial(back_kernel, shift),
        in_specs=[pl.BlockSpec(memory_space=pltpu.VMEM)] * 3,
        out_shape=[
            jax.ShapeDtypeStruct((count, width), BF16),
            jax.ShapeDtypeStruct((width, width), F32),
        ],
        compiler_params=params(),
        cost_estimate=cost(4 * count * width * width, 6 * count * width),
        name="back",
    )(got, sums, square)


def own_kernel(nodes, done, count, weights_ref, scaled_ref, got_ref, matrix_ref, own_ref, inverse_ref):
    width = inverse_ref.shape[0]
    each = width // STEPS

    @pl.when(pl.program_id(0) == 0)
    def _():
        matrix = matrix_ref[...]
        inverse_ref[...] = matrix if done else matrix * (1.0 / nodes)

    for step in range(count):

        @pl.when(pl.program_id(0) == step)
        def _():
            own_ref[...] = scaled_ref[...] - dot(weights_ref[...], got_ref[...])
            start = (done + step) * each
            inverse_ref[...] = eliminate(inverse_ref[...], start, each)


def eliminate(matrix, start, count, some=4):
    rows = lax.broadcasted_iota(jnp.int32, matrix.shape, 0)
    lanes = lax.broadcasted_iota(jnp.int32, matrix.shape, 1)
    for first in range(start, start + count, some):
        columns = [
            jnp.broadcast_to(matrix[:, k:k + 1], matrix.shape) for k in range(first, first + some)
        ]
        for at, k in enumerate(range(first, first + some)):
            here, column = rows == k, columns[at]
            pivot = 1.0 / column[k:k + 1, :]
            scaled = jnp.where(lanes[:1] == k, pivot, matrix[k:k + 1, :] * pivot)
            rest = jnp.where(lanes == k, 0.0, matrix) - column * scaled
            matrix = jnp.where(here, scaled, rest)
            for later in range(at + 1, some):
                value = columns[later][k:k + 1, :] * pivot
                columns[later] = jnp.where(here, value, columns[later] - column * value)
    return matrix


def own_of(weights, scaled, got, matrix, nodes, done, steps, skip, tile):
    count, width = got.shape
    rows = steps * tile
    return pl.pallas_call(
        functools.partial(own_kernel, nodes, done, steps),
        grid=(steps,),
        in_specs=[
            pl.BlockSpec((tile, count), lambda i: (i + skip, 0)),
            pl.BlockSpec((tile, width), lambda i: (i + skip, 0)),
            pl.BlockSpec(memory_space=pltpu.VMEM),
            pl.BlockSpec((width, width), lambda i: (0, 0)),
        ],
        out_specs=[
            pl.BlockSpec((tile, width), lambda i: (i, 0)),
            pl.BlockSpec((width, width), lambda i: (0, 0)),
        ],
        out_shape=[
            jax.ShapeDtypeStruct((rows, width), F32),
            jax.ShapeDtypeStruct((width, width), F32),
        ],
        compiler_params=params(),
        cost_estimate=cost(2 * rows * count * width, 2 * rows * count),
        name="own",
    )(weights, scaled, got, matrix)


def split(value):
    first = value.astype(BF16)
    return first, (value - first.astype(F32)).astype(BF16)


def set_right(nodes, scale, inverse_ref, spread_ref, right_ref):
    width = inverse_ref.shape[0]
    high = lax.Precision.HIGHEST
    inverse = inverse_ref[...]
    half = jnp.dot(inverse, spread_ref[...], precision=high, preferred_element_type=F32)
    sandwich = jnp.dot(half, inverse, precision=high, preferred_element_type=F32)
    for at, value in ((0, 2.0 * scale * inverse), (width, -2.0 * scale / nodes * sandwich)):
        first, second = split(value)
        right_ref[at:at + width, :width] = first
        right_ref[at:at + width, width:] = second


def grad_y_rows(shift, start, own, y, index, returned, right_ref):
    tile, width = y.shape
    at = lax.broadcasted_iota(jnp.int32, (tile, returned.shape[0]), 0) + start
    spots = jnp.where(at == index, 1.0, 0.0)
    times = jnp.sum(spots, axis=1, keepdims=True)
    nearby = own + dot(spots.astype(BF16), returned) + shift * times * y
    first, second = split(nearby)
    y_first, y_second = split(y)
    both = dot(jnp.concatenate([first, y_first], axis=1), right_ref[...])
    rest = dot(jnp.concatenate([second, y_second], axis=1), right_ref[:, :width])
    return (both[:, :width] + both[:, width:] + rest).astype(BF16)


def grad_y_kernel(nodes, scale, shift, places, *refs):
    parts = len(places)
    own_refs = refs[:parts]
    y_ref, index_ref, returned_ref, inverse_ref, spread_ref, out_ref, right_ref = refs[parts:]
    tile = y_ref.shape[0]

    @pl.when(pl.program_id(0) == 0)
    def _():
        set_right(nodes, scale, inverse_ref, spread_ref, right_ref)

    for place, own_ref in zip(places, own_refs):

        @pl.when(in_span(*place))
        def _():
            out_ref[...] = grad_y_rows(
                shift, pl.program_id(0) * tile, own_ref[...], y_ref[...], index_ref[...],
                returned_ref[...], right_ref
            )


def spans(arrays, tile):
    result, first = [], 0
    for x in arrays:
        result.append((first, x.shape[0] // tile))
        first += x.shape[0] // tile
    return result


def span_block(tile, width, first, each):
    return pl.BlockSpec((tile, width), lambda i: (jnp.clip(i - first, 0, each - 1), 0))


def in_span(first, each):
    return (pl.program_id(0) >= first) & (pl.program_id(0) < first + each)


def grad_y_of(own, y, send_rows, returned, inverse, spread, shift, nodes, scale):
    rows, width = y.shape
    count = returned.shape[0]
    tile = min(512, own[0].shape[0])
    places = spans(own, tile)
    return pl.pallas_call(
        functools.partial(grad_y_kernel, nodes, scale, shift, places),
        grid=(rows // tile,),
        in_specs=[span_block(tile, width, *place) for place in places]
        + [
            pl.BlockSpec((tile, width), lambda i: (i, 0)),
            pl.BlockSpec((1, count), lambda i: (0, 0)),
            pl.BlockSpec((count, width), lambda i: (0, 0)),
            pl.BlockSpec((width, width), lambda i: (0, 0)),
            pl.BlockSpec((width, width), lambda i: (0, 0)),
        ],
        out_specs=pl.BlockSpec((tile, width), lambda i: (i, 0)),
        out_shape=jax.ShapeDtypeStruct((rows, width), BF16),
        scratch_shapes=[pltpu.VMEM((2 * width, 2 * width), BF16)],
        compiler_params=params(),
        cost_estimate=cost(2 * rows * count * width, 8 * rows * width),
        name="grad_y",
    )(*own, y, send_rows.reshape(1, count), returned, inverse, spread)


def radices(n):
    result, shift = [], 0
    while 1 << shift < n:
        bits = 1 if shift == 0 else min(2, n.bit_length() - 1 - shift)
        result.append((shift, 1 << bits))
        shift += bits
    return result


def position(relative, n):
    total = 0
    for shift, radix in radices(n):
        total = total * radix + ((relative >> shift) & (radix - 1))
    return total


def add_grads(x_ref, hidden_ref, slope_ref, gy, w_out_ref, g_in, g_out):
    units = g_in.shape[1]
    step = min(512, units)
    x = x_ref[...]
    for at in range(0, units, step):
        back = dot_nt(gy, w_out_ref[at:at + step, :])
        grad = (back * slope_ref[:, at:at + step]).astype(BF16)
        g_in[:, at:at + step] += dot_tn(x, grad)
    g_out[...] += dot_tn(hidden_ref[...], gy)


def backward_kernel(x_ref, hidden_ref, slope_ref, gy_ref, w_out_ref, g_in, g_out):
    @pl.when(pl.program_id(0) == 0)
    def _():
        g_in[...] = jnp.zeros_like(g_in)
        g_out[...] = jnp.zeros_like(g_out)

    add_grads(x_ref, hidden_ref, slope_ref, gy_ref[...], w_out_ref, g_in, g_out)


def backward(features, hidden, slope, gy, w_out):
    nodes, din = features.shape
    units, width = w_out.shape
    tile = min(1024, nodes)
    shapes = [
        jax.ShapeDtypeStruct((din, units), F32),
        jax.ShapeDtypeStruct((units, width), F32),
    ]
    return pl.pallas_call(
        backward_kernel,
        grid=(nodes // tile,),
        in_specs=[
            pl.BlockSpec((tile, din), lambda i: (i, 0)),
            pl.BlockSpec((tile, units), lambda i: (i, 0)),
            pl.BlockSpec((tile, units), lambda i: (i, 0)),
            pl.BlockSpec((tile, width), lambda i: (i, 0)),
            pl.BlockSpec((units, width), lambda i: (0, 0)),
        ],
        out_specs=[pl.BlockSpec(x.shape, lambda i: (0, 0)) for x in shapes],
        out_shape=shapes,
        compiler_params=params(),
        cost_estimate=cost(2 * nodes * units * (din + 2 * width), 2 * nodes * (din + 3 * units)),
        name="backward",
    )(features, hidden, slope, gy, w_out)


def packed_kernel(nodes, scale, shift, n, places, *refs):
    parts = len(places)
    own_refs = refs[:parts]
    y_ref, index_ref, returned_ref, inverse_ref, spread_ref = refs[parts:parts + 5]
    x_ref, hidden_ref, slope_ref, w_out_ref, me_ref = refs[parts + 5:parts + 10]
    *outs, g_in, g_out, gy_ref, right_ref = refs[parts + 10:]
    tile = y_ref.shape[0]
    some = min(512, tile)

    @pl.when(pl.program_id(0) == 0)
    def _():
        set_right(nodes, scale, inverse_ref, spread_ref, right_ref)
        g_in[...] = jnp.zeros_like(g_in)
        g_out[...] = jnp.zeros_like(g_out)

    for place, own_ref in zip(places, own_refs):

        @pl.when(in_span(*place))
        def _():
            for at in range(0, tile, some):
                gy_ref[at:at + some, :] = grad_y_rows(
                    shift, pl.program_id(0) * tile + at, own_ref[at:at + some, :],
                    y_ref[at:at + some, :], index_ref[...], returned_ref[...], right_ref
                )

    add_grads(x_ref, hidden_ref, slope_ref, gy_ref[...], w_out_ref, g_in, g_out)

    @pl.when(pl.program_id(0) == pl.num_programs(0) - 1)
    def _():
        me = me_ref[0]
        units = g_in.shape[1]
        chunk = g_in.shape[0] // n
        for pair in range(n // 2):
            for side, out in enumerate(outs):
                c = 2 * pair + (me + side) % 2
                at = pl.multiple_of((position(me ^ c, n) % (n // 2)) * chunk, chunk)
                rows = pl.ds(pl.multiple_of(c * chunk, chunk), chunk)
                out[pl.ds(at, chunk), :units] = g_in[rows, :].astype(out.dtype)
                out[pl.ds(at, chunk), units:] = g_out[rows, :].astype(out.dtype)


def packed_grads(
    own, y, send_rows, returned, inverse, spread, features, hidden, slope, w_out, me,
    nodes, scale, shift, n
):
    rows, din = features.shape
    units, width = w_out.shape
    count = returned.shape[0]
    tile = min(1024, own[0].shape[0])
    places = spans(own, tile)
    shapes = [
        jax.ShapeDtypeStruct((din // 2, units + width), F32),
        jax.ShapeDtypeStruct((din // 2, units + width), BF16),
    ]
    return pl.pallas_call(
        functools.partial(packed_kernel, nodes, scale, shift, n, places),
        grid=(rows // tile,),
        in_specs=[span_block(tile, width, *place) for place in places]
        + [
            pl.BlockSpec((tile, width), lambda i: (i, 0)),
            pl.BlockSpec((1, count), lambda i: (0, 0)),
            pl.BlockSpec(memory_space=pltpu.VMEM),
            pl.BlockSpec((width, width), lambda i: (0, 0)),
            pl.BlockSpec((width, width), lambda i: (0, 0)),
            pl.BlockSpec((tile, din), lambda i: (i, 0)),
            pl.BlockSpec((tile, units), lambda i: (i, 0)),
            pl.BlockSpec((tile, units), lambda i: (i, 0)),
            pl.BlockSpec((units, width), lambda i: (0, 0)),
            pl.BlockSpec(memory_space=pltpu.SMEM),
        ],
        out_specs=[pl.BlockSpec(x.shape, lambda i: (0, 0)) for x in shapes],
        out_shape=shapes,
        scratch_shapes=[
            pltpu.VMEM((din, units), F32),
            pltpu.VMEM((units, width), F32),
            pltpu.VMEM((tile, width), BF16),
            pltpu.VMEM((2 * width, 2 * width), BF16),
        ],
        compiler_params=params(50),
        cost_estimate=cost(2 * rows * units * (din + 2 * width), 2 * rows * (din + 3 * units)),
        name="packed_grads",
    )(
        *own, y, send_rows.reshape(1, count), returned, inverse, spread,
        features, hidden, slope, w_out, me
    )


def unpack_kernel(places, lows, me_ref, *refs):
    *pieces, g_in_ref, g_out_ref = refs
    chunk, units = g_in_ref.shape[2:]
    half = len(pieces) // 2
    for k in range(half):

        @pl.when(pl.program_id(0) == k)
        def _():
            for side, piece in enumerate((pieces[k], pieces[half + k])):
                for t, place in enumerate(places):
                    part = piece[t * chunk:(t + 1) * chunk, :].astype(F32)
                    at = place ^ (me_ref[0] // lows)
                    g_in_ref[at, (me_ref[0] + side) % 2] = part[:, :units]
                    g_out_ref[at, (me_ref[0] + side) % 2] = part[:, units:]


def unpack(pieces, spots, places, lows, me, shapes):
    held = pl.BlockSpec(memory_space=pltpu.VMEM)

    def spot(i, me_ref):
        value = sum(jnp.where(i == k, x // 2, 0) for k, x in enumerate(spots))
        return 0, value ^ (me_ref[0] % lows // 2), 0, 0

    return pl.pallas_call(
        functools.partial(unpack_kernel, places, lows),
        grid_spec=pltpu.PrefetchScalarGridSpec(
            num_scalar_prefetch=1,
            grid=(len(pieces) // 2,),
            in_specs=[held] * len(pieces),
            out_specs=[pl.BlockSpec((x.shape[0], 2) + x.shape[2:], spot) for x in shapes],
        ),
        out_shape=shapes,
        compiler_params=params(12),
        cost_estimate=cost(1e9, 0),
        name="unpack",
    )(me, *pieces)


def exchange(value, axis, n, mask):
    return lax.ppermute(value, axis, [(i, i ^ mask) for i in range(n)])


def sum_step(value, axis, n, step, after=None):
    if step is None:
        return lax.psum(value, axis)
    shift, radix = step
    got = [exchange(value, axis, n, m << shift) for m in range(1, radix)]
    if after is not None:
        got, _ = lax.optimization_barrier((got, after))
    return sum(got, value)


def reduce_step(value, axis, n, step):
    shift, radix = step
    size = value.shape[0] // radix
    total = value[:size]
    for m in range(1, radix):
        part = value[m * size:(m + 1) * size].astype(BF16)
        total = total + exchange(part, axis, n, m << shift).astype(F32)
    return total


def gather_unpack(value, axis, n, me, units):
    steps = radices(n)
    for shift, radix in reversed(steps[2:]):
        parts = [value] + [exchange(value, axis, n, m << shift) for m in range(1, radix)]
        value = jnp.concatenate(parts, axis=0)
    shift, radix = steps[1]
    lows = 2 * radix
    rest = n // lows
    chunk = value.shape[0] // rest
    both = value.shape[1]
    shapes = [
        jax.ShapeDtypeStruct((rest, lows, chunk, size), F32) for size in (units, both - units)
    ]
    places = sorted(range(rest), key=lambda r: position(r * lows, n))
    order = sorted(range(radix), key=lambda m: bin(m).count("1"))
    here = [exchange(value, axis, n, m << shift) if m else value for m in order]
    there = [exchange(piece, axis, n, 1) for piece in here]
    pieces = here + there
    spots = [m << shift for m in order]
    outs = unpack(pieces, spots, places, lows, me, shapes)
    return tuple(x.reshape(n * chunk, -1) for x in outs)


def shards(features, w_in, w_out, send_rows, pair_src, pair_weight, pair_mask):
    n_dp = lax.axis_size("dp")
    n_mp = lax.axis_size("mp")
    group_rows, din = features.shape
    nodes = group_rows * n_dp
    rows = group_rows // n_mp
    units, width = w_out.shape
    pairs = pair_src.shape[1]
    count = send_rows.shape[0]
    scale = 1.0 / (pairs * math.sqrt(nodes))
    me = lax.axis_index("dp").astype(jnp.int32).reshape(1)

    per = 256
    src = pair_src.reshape(rows * pairs // per, per)
    coef = (pair_weight * pair_mask.astype(F32)).reshape(rows * pairs // per, per)

    steps = [None] if n_dp & (n_dp - 1) else radices(n_dp)
    hidden, slope, y, rounded, gram = forward(features, w_in, w_out)
    if n_mp > 1:
        y = lax.psum_scatter(y, "mp", scatter_dimension=0, tiled=True)
        rounded = y.astype(BF16)
        gram = lax.psum(dot_tn(rounded, rounded), "mp")
    sent = send(y, send_rows)
    got = lax.all_to_all(sent, "dp", split_axis=0, concat_axis=0, tiled=True)
    parts = 2 if rows % (2 * 512) == 0 else 1
    weights, scaled, carry = [], [], ()
    for part in range(parts):
        if steps:
            gram = sum_step(gram, "dp", n_dp, steps[0], sent if part == 0 else None)
            steps = steps[1:]
            gram, rounded, carry = lax.optimization_barrier((gram, rounded, carry))
        piece, with_y, *carry = weights_of(
            src, coef, y, rounded, carry, pairs, count, part, parts
        )
        weights.append(piece)
        scaled.append(with_y)
    for step in steps:
        gram = sum_step(gram, "dp", n_dp, step, carry[1])
    gram, carry = lax.optimization_barrier((gram, carry))
    shift = SHIFT * pairs * rows / count
    back, spread = back_of(got, *carry, shift)
    returned = lax.all_to_all(back, "dp", split_axis=0, concat_axis=0, tiled=True)
    matrix, _ = lax.optimization_barrier((gram, back))
    own, marks = [], []
    half = STEPS // parts
    some = STEPS // 4
    cuts = [(0, some), (some, some), (half, half)] if parts == 2 else [(0, STEPS)]
    for done, taken in cuts:
        part, skip = divmod(done, half)
        piece, matrix = own_of(
            weights[part], scaled[part], got, matrix, nodes, done, taken, skip, rows // STEPS
        )
        own.append(piece)
        marks.append(matrix)
    steps = [None] if n_dp & (n_dp - 1) else radices(n_dp)
    for k, step in enumerate(steps):
        spread = sum_step(spread, "dp", n_dp, step, marks[min(k, len(marks) - 1)])
    if n_mp > 1:
        spread = lax.psum(spread, "mp")
    packable = n_dp & (n_dp - 1) == 0 and n_dp > 2 and din == units and din % (16 * n_dp) == 0
    if not packable or n_mp > 1:
        gy = grad_y_of(own, y, send_rows, returned, matrix, spread, shift, nodes, scale)
        if n_mp > 1:
            gy = lax.all_gather(gy, "mp", axis=0, tiled=True)
        return lax.psum(tuple(backward(features, hidden, slope, gy, w_out)), "dp")
    kept, given = packed_grads(
        own, y, send_rows, returned, matrix, spread, features, hidden, slope, w_out, me,
        nodes, scale, shift, n_dp
    )
    value = kept + exchange(given, "dp", n_dp, 1).astype(F32)
    for step in radices(n_dp)[1:]:
        value = reduce_step(value, "dp", n_dp, step)
    return gather_unpack(value.astype(BF16), "dp", n_dp, me, units)


def solution(mesh):
    return jax.shard_map(
        shards,
        mesh=mesh,
        in_specs=(
            P("dp", None),
            P(None, "mp"),
            P("mp", None),
            P(("dp", "mp")),
            P(("dp", "mp"), None),
            P(("dp", "mp"), None),
            P(("dp", "mp"), None),
        ),
        out_specs=(P(None, "mp"), P("mp", None)),
        check_vma=False,
    )
```
